512 devices in a mesh: section: 8 (over y, core), expert: 64 (over x, z).
Axes of the slice: x: 4, y: 4, z: 16, core: 2. Of those that a mesh axis runs over, the one named last changes fastest.
Arguments:
- fwd_input: bfloat16 [8, 1024, 3584], P('section', 'expert'), may hold values from -6 to 6
- fwd_ids: int32 [8, 1024, 2], P('section', 'expert'), may hold values from 0 to 7, all different within a row; in each aligned block of 16 rows (0 to 15, 16 to 31, ..., all dimensions but the last counted through in order) at most 6 rows name the same one
- bwd_input: bfloat16 [8, 1024, 3584], P('section', 'expert'), may hold values from -6 to 6
- bwd_ids: int32 [8, 1024, 2], P('section', 'expert'), may hold values from 0 to 7, all different within a row; in each aligned block of 16 rows (0 to 15, 16 to 31, ..., all dimensions but the last counted through in order) at most 6 rows name the same one
- bwd_cot: bfloat16 [8, 1024, 3584], P('section', 'expert'), may hold values from -6 to 6
- centroids: bfloat16 [8, 8, 3584], P('section'), may hold values from -0.09375 to 0.09375
- w_gate: bfloat16 [8, 3584, 8192], P('section', None, 'expert'), may hold values from -0.09375 to 0.09375
- w_up: bfloat16 [8, 3584, 8192], P('section', None, 'expert'), may hold values from -0.09375 to 0.09375
- w_down: bfloat16 [8, 8192, 3584], P('section', 'expert'), may hold values from -0.1875 to 0.1875
Outputs:
- fwd_out: bfloat16 [8, 1024, 3584], P('section', 'expert')
- bwd_out: bfloat16 [8, 1024, 3584], P('section', 'expert')
The draws below stay inside these ranges and needn't reach their ends.
Inputs may be any that keep to these rules, and one draw needn't show every extreme that they name: `fwd_ids`: each row names 2 different experts. Among the 16 rows of one device at one layer, at most 6 name the same expert, a bound that some block reaches in every draw. `bwd_ids`: as fwd_ids.
All inputs are finite; a program needn't handle non-finite values.
Results may differ from the reference program's by a relative error of at most 0.0075.
Values may be sent and summed in bfloat16 or wider, within the bound.
A program may use at most 64 MiB of HBM per device.

```python
import math
import jax
import jax.numpy as jnp
import numpy as np
from jax import lax

D = 3584
FF = 1024
EF = 8
TOP = 2
TOK = 16
CAP = 6
SHARDS = 8
FF_DEV = 128
TOKENS = 1024
LAYERS = 8
N_EXPERT = 64


def block_scale(stream_key, dims, pieces, smallest, top_value):
    level = 1.0
    for axis_at, blocks in pieces:
        heights = jax.random.uniform(jax.random.fold_in(jax.random.fold_in(stream_key, 6), axis_at), (blocks,), jnp.float32, smallest / len(pieces), top_value / len(pieces))
        level = level * jnp.repeat(jnp.exp(heights), dims[axis_at] // blocks).reshape((-1,) + (1,) * (len(dims) - 1 - axis_at))
    return level


def assign_block(own_key, own, number, rows, number_of, top, bound, slope):
    sequence = jax.random.permutation(own_key, number_of)
    heavy_load, ordinary = portions_of(number_of, rows * top, bound, slope, True), portions_of(number_of, rows * top, bound, slope, False)
    places = jnp.arange(number_of)

    def named(sizes, offset_by):
        used = int((sizes > 0).sum())
        fixed = max(1, used // 4)
        moved = fixed + (places - fixed + offset_by * (used - fixed)) % max(1, number_of - fixed)
        return jnp.zeros((number_of,), jnp.int32).at[sequence[jnp.where(places < fixed, places, moved)]].set(jnp.asarray(sizes, jnp.int32))

    sizes = jnp.where(number % 4 == 0, named(heavy_load, number // 4), named(ordinary, number - number // 4 - 1))
    mixed = jax.random.permutation(jax.random.fold_in(own, 3), number_of)
    giver, taker = mixed[0:number_of // 2 * 2:2], mixed[1:number_of // 2 * 2:2]
    slack = jnp.minimum(sizes[giver] - 1, bound - sizes[taker]) // 2
    slack = jnp.where((giver == sequence[0]) | (taker == sequence[0]) | (sizes[taker] == 0), 0, jnp.maximum(slack, 0))
    moved = jax.random.randint(jax.random.fold_in(own, 4), (number_of // 2,), 0, 1 << 20) % (slack + 1)
    sizes = sizes.at[giver].add(-moved).at[taker].add(moved)
    items = jnp.searchsorted(jnp.cumsum(sizes), jnp.arange(rows * top), side="right").astype(jnp.int32)
    table = items.reshape(top, rows).T
    table = table[jax.random.permutation(jax.random.fold_in(own, 1), rows)]
    offset_by = jax.random.randint(jax.random.fold_in(own, 2), (rows, 1), 0, top)
    return jnp.take_along_axis(table, (jnp.arange(top)[None, :] + offset_by) % top, axis=1)


def portions_of(count, total, reach, slope, full):
    portions = [(1 << 20) // math.isqrt(grade ** slope) + 1 for grade in range(1, count + 1)]
    largest = reach if full else min(reach, max(-(-total // count), total * portions[0] // sum(portions)))
    least = 1 if total - largest >= count - 1 else 0
    holding, surplus = [largest] + [least] * (count - 1), total - largest - least * (count - 1)
    while surplus > 0:
        free = [i for i in range(1, count) if holding[i] < largest] or [i for i in range(1, count) if holding[i] < reach]
        whole, left = sum([portions[i] for i in free]), surplus
        for i in free:
            more = min(reach - holding[i], max(1, left * portions[i] // whole), surplus)
            holding[i] = holding[i] + more
            surplus = surplus - more
    return np.array(holding)


def bell_draw(stream_key, extent, deviation, bound, pieces=(), kind=jnp.bfloat16):
    values = deviation * jax.random.normal(stream_key, extent, jnp.float32)
    if pieces:
        values = values * block_scale(stream_key, extent, pieces, -0.22, 0.18)
    return jnp.clip(values, -bound, bound).astype(kind)


def setup_inputs(seed: int = 0) -> dict:
    key_of = jax.random.split(jax.random.key(seed), 10)
    fwd_input = bell_draw(key_of[0], (LAYERS, TOKENS, D), 1.0, 6.0, ((0, 8), (1, 64)))
    fwd_ids_keys = jax.random.split(jax.random.fold_in(key_of[1], 1), LAYERS * TOKENS // TOK)
    fwd_ids_turns = jax.random.permutation(jax.random.fold_in(key_of[1], 3), LAYERS * TOKENS // TOK)
    fwd_ids = jax.vmap(lambda own, number: assign_block(jax.random.fold_in(key_of[1], 2), own, number, TOK, EF, TOP, CAP, 2))(fwd_ids_keys, fwd_ids_turns).reshape((LAYERS, TOKENS, TOP))
    bwd_input = bell_draw(key_of[2], (LAYERS, TOKENS, D), 1.0, 6.0, ((0, 8), (1, 64)))
    bwd_ids_keys = jax.random.split(jax.random.fold_in(key_of[3], 1), LAYERS * TOKENS // TOK)
    bwd_ids_turns = jax.random.permutation(jax.random.fold_in(key_of[3], 3), LAYERS * TOKENS // TOK)
    bwd_ids = jax.vmap(lambda own, number: assign_block(jax.random.fold_in(key_of[3], 2), own, number, TOK, EF, TOP, CAP, 2))(bwd_ids_keys, bwd_ids_turns).reshape((LAYERS, TOKENS, TOP))
    bwd_cot = bell_draw(key_of[4], (LAYERS, TOKENS, D), 1.0, 6.0, ((0, 8), (1, 64)))
    centroids = bell_draw(key_of[5], (LAYERS, EF, D), D ** -0.5, 0.09375, ((0, 8),))
    w_gate = bell_draw(key_of[6], (LAYERS, D, EF * FF), D ** -0.5, 0.09375, ((0, 8), (2, 64)))
    w_up = bell_draw(key_of[7], (LAYERS, D, EF * FF), D ** -0.5, 0.09375, ((0, 8), (2, 64)))
    w_down = bell_draw(key_of[8], (LAYERS, EF * FF, D), FF ** -0.5, 0.1875, ((0, 8), (1, 64)))
    return {"fwd_input": fwd_input, "fwd_ids": fwd_ids, "bwd_input": bwd_input, "bwd_ids": bwd_ids, "bwd_cot": bwd_cot, "centroids": centroids, "w_gate": w_gate, "w_up": w_up, "w_down": w_down}


EPS = 1e-06
ROUTE_SCALE = 2.5

def normalize_rows(values):
    widened = values.astype(jnp.float32)
    inverse = lax.rsqrt(lax.optimization_barrier(jnp.mean(widened * widened, axis=-1, keepdims=True)) + EPS)
    return (widened, inverse, (widened * inverse).astype(jnp.bfloat16))

def router_gates(normed, route_ids, centre_w):
    logits = lax.dot_general(normed, centre_w, (((1,), (1,)), ((), ())), preferred_element_type=jnp.float32)
    chosen_hot = (route_ids[..., None] == jnp.arange(EF, dtype=jnp.int32)).astype(jnp.float32)
    chosen = lax.optimization_barrier(jnp.sum(chosen_hot * logits[:, None, :], axis=-1))
    affinity = jax.nn.sigmoid(chosen)
    affinity_sum = lax.optimization_barrier(jnp.sum(affinity, axis=-1, keepdims=True))
    return (chosen_hot, affinity, affinity_sum, affinity / affinity_sum)

def slot_places(route_ids):
    flat_ids = route_ids.reshape(-1)
    slot_hits = (flat_ids[:, None] == jnp.arange(EF, dtype=jnp.int32)).astype(jnp.int32)
    earlier = jnp.cumsum(slot_hits, axis=0, dtype=jnp.int32) - slot_hits
    slot_index = lax.optimization_barrier(jnp.sum(earlier * slot_hits, axis=-1, dtype=jnp.int32))
    return (flat_ids * CAP + slot_index).reshape(route_ids.shape)

def slot_tables(route_ids):
    places = jax.vmap(slot_places)(route_ids.reshape(N_EXPERT, TOK, TOP))
    return (places[..., None] == jnp.arange(EF * CAP, dtype=jnp.int32)).astype(jnp.float32)

def dispatch(slot_table, values):
    flat_table = lax.optimization_barrier(jnp.sum(slot_table, axis=2))
    spread = jnp.einsum('ntq,ntd->nqd', flat_table, values.reshape(N_EXPERT, TOK, D).astype(jnp.float32), precision=lax.Precision.HIGHEST)
    return spread.astype(jnp.bfloat16)

def round_trip(values):
    return lax.optimization_barrier(values.astype(jnp.bfloat16)).astype(jnp.float32)

def expert_forward(in_rows, gate_w, up_w, down_w):
    gate_pre = jnp.dot(in_rows, gate_w, preferred_element_type=jnp.float32)
    up_pre = jnp.dot(in_rows, up_w, preferred_element_type=jnp.float32)
    hidden_act = (gate_pre * jax.nn.sigmoid(gate_pre) * up_pre).astype(jnp.bfloat16)
    summed = jnp.zeros((in_rows.shape[0], D), jnp.float32)
    for shard_index in range(SHARDS):
        low_col = shard_index * FF_DEV
        part_out = jnp.dot(hidden_act[:, low_col:low_col + FF_DEV], down_w[low_col:low_col + FF_DEV], preferred_element_type=jnp.float32)
        summed = summed + round_trip(part_out)
    return summed

def contract_cols(left, right):
    return lax.dot_general(left, right, (((1,), (1,)), ((), ())), preferred_element_type=jnp.float32)

def expert_backward(in_rows, grad_rows, gate_w, up_w, down_w):
    gate_pre = jnp.dot(in_rows, gate_w, preferred_element_type=jnp.float32)
    up_pre = jnp.dot(in_rows, up_w, preferred_element_type=jnp.float32)
    gate_sig = jax.nn.sigmoid(gate_pre)
    hidden_act = (gate_pre * gate_sig * up_pre).astype(jnp.bfloat16)
    grad_act = contract_cols(grad_rows, down_w)
    inner_terms = hidden_act.astype(jnp.float32) * grad_act
    grad_gate = (grad_act * up_pre * gate_sig * (1.0 + gate_pre * (1.0 - gate_sig))).astype(jnp.bfloat16)
    grad_up = (grad_act * gate_pre * gate_sig).astype(jnp.bfloat16)
    grad_sum = jnp.zeros((in_rows.shape[0], D), jnp.float32)
    dot_sum = jnp.zeros((in_rows.shape[0],), jnp.float32)
    for shard_index in range(SHARDS):
        low_col = shard_index * FF_DEV
        high_col = low_col + FF_DEV
        term = contract_cols(grad_gate[:, low_col:high_col], gate_w[:, low_col:high_col])
        term = term + contract_cols(grad_up[:, low_col:high_col], up_w[:, low_col:high_col])
        grad_sum = grad_sum + round_trip(term)
        dot_sum = dot_sum + round_trip(lax.optimization_barrier(jnp.sum(inner_terms[:, low_col:high_col], axis=-1)))
    return (grad_sum, dot_sum)

def expert_block(layer_index, expert_index, w_gate, w_up, w_down):
    low_col = expert_index * FF
    return (w_gate[layer_index][:, low_col:low_col + FF], w_up[layer_index][:, low_col:low_col + FF], w_down[layer_index][low_col:low_col + FF])

def layer_forward(layer_index, values, route_ids, centroids, w_gate, w_up, w_down):
    widened, inverse, normed = normalize_rows(values)
    chosen_hot, affinity, affinity_sum, gate_share = router_gates(normed, route_ids, centroids[layer_index])
    slot_table = slot_tables(route_ids)
    sent = dispatch(slot_table, normed)
    outputs = []
    for expert_index in range(EF):
        gate_w, up_w, down_w = expert_block(layer_index, expert_index, w_gate, w_up, w_down)
        in_rows = sent[:, expert_index * CAP:(expert_index + 1) * CAP].reshape(-1, D)
        outputs.append(expert_forward(in_rows, gate_w, up_w, down_w).reshape(N_EXPERT, CAP, D))
    summed = jnp.concatenate(outputs, axis=1)
    mixing = lax.optimization_barrier(jnp.sum(ROUTE_SCALE * gate_share.reshape(N_EXPERT, TOK, TOP)[..., None] * slot_table, axis=2))
    routed = jnp.einsum('ntq,nqd->ntd', mixing, summed, precision=lax.Precision.HIGHEST)
    return (widened + routed.reshape(TOKENS, D)).astype(jnp.bfloat16)

def layer_backward(layer_index, values, route_ids, cotangent, centroids, w_gate, w_up, w_down):
    widened, inverse, normed = normalize_rows(values)
    centre_w = centroids[layer_index]
    chosen_hot, affinity, affinity_sum, gate_share = router_gates(normed, route_ids, centre_w)
    slot_table = slot_tables(route_ids)
    sent_h = dispatch(slot_table, normed)
    sent_g = dispatch(slot_table, cotangent)
    grads = []
    dots = []
    for expert_index in range(EF):
        gate_w, up_w, down_w = expert_block(layer_index, expert_index, w_gate, w_up, w_down)
        low_row = expert_index * CAP
        in_rows = sent_h[:, low_row:low_row + CAP].reshape(-1, D)
        grad_rows = sent_g[:, low_row:low_row + CAP].reshape(-1, D)
        grad_sum, dot_sum = expert_backward(in_rows, grad_rows, gate_w, up_w, down_w)
        grads.append(grad_sum.reshape(N_EXPERT, CAP, D))
        dots.append(dot_sum.reshape(N_EXPERT, CAP))
    summed = jnp.concatenate(grads, axis=1)
    dot_sums = jnp.concatenate(dots, axis=1)
    gate_dots = jnp.einsum('ntkq,nq->ntk', slot_table, dot_sums, precision=lax.Precision.HIGHEST).reshape(TOKENS, TOP)
    scaled = ROUTE_SCALE * gate_dots
    centre = lax.optimization_barrier(jnp.sum(gate_share * scaled, axis=-1, keepdims=True))
    gate_slope = (scaled - centre) / affinity_sum * affinity * (1.0 - affinity)
    mixing = lax.optimization_barrier(jnp.sum(ROUTE_SCALE * gate_share.reshape(N_EXPERT, TOK, TOP)[..., None] * slot_table, axis=2))
    grad_normed = jnp.einsum('ntq,nqd->ntd', mixing, summed, precision=lax.Precision.HIGHEST).reshape(TOKENS, D)
    slope_full = lax.optimization_barrier(jnp.sum(gate_slope[..., None] * chosen_hot, axis=1))
    grad_normed = grad_normed + jnp.dot(slope_full, centre_w.astype(jnp.float32), precision=lax.Precision.HIGHEST)
    projection = lax.optimization_barrier(jnp.mean(grad_normed * widened, axis=-1, keepdims=True))
    result = cotangent.astype(jnp.float32) + inverse * grad_normed - inverse * inverse * inverse * widened * projection
    return result.astype(jnp.bfloat16)

def reference(fwd_input, fwd_ids, bwd_input, bwd_ids, bwd_cot, centroids, w_gate, w_up, w_down):
    forward_list = []
    backward_list = []
    for layer_index in range(LAYERS):
        carried = fwd_input[(layer_index - 1) % LAYERS]
        forward_list.append(layer_forward(layer_index, carried, fwd_ids[layer_index], centroids, w_gate, w_up, w_down))
        backward_list.append(layer_backward(layer_index, bwd_input[layer_index], bwd_ids[layer_index], bwd_cot[layer_index], centroids, w_gate, w_up, w_down))
    return (jnp.stack(forward_list), jnp.stack(backward_list))
```

```python
import functools

import jax
import jax.numpy as jnp
from jax import lax
from jax.experimental import pallas as pl
from jax.experimental.pallas import tpu as pltpu
from jax.sharding import PartitionSpec as P

MESH = pl.DeviceIdType.MESH
EF = 8
CAP = 6
NX = 4
NZ = 16
TOK = 16
EPS = 1e-06
ROUTE_SCALE = 2.5
NC = 2
GROUP = NZ // 2
SLOTS = GROUP * CAP
ROWS = NX * SLOTS
GT = GROUP * TOK
LANES = 128
STEP = 256
DEPTH = 512
F32 = jnp.float32
BF16 = jnp.bfloat16
NT = (((1,), (1,)), ((), ()))


def dot(a, b):
    return jnp.dot(a, b, preferred_element_type=F32)


def dot_nt(a, b):
    return lax.dot_general(a, b, NT, preferred_element_type=F32)


def sigmoid(v):
    return jax.nn.sigmoid(v)


def kernel(
    fx_ref, fid_ref, bx_ref, bid_ref, dy_ref, cent_ref, wg_ref, wu_ref, wd_ref,
    outf_ref, outb_ref,
    wgu, wdv, cpad, rx, zm, zb, tt, tu, thi, tlo, xs, xr, yr, ys, ypr, yps, pacc, pp, rss, rsr, rps, rpr, uvb,
    wsem, shs, shr, zms, zmr, zs, zr, xss, xrs, yss, yrs, ypss, yprs, rsss, rsrs, rpss, rprs,
):
    D = fx_ref.shape[-1]
    DC = D // NC
    FF = wdv.shape[0]
    sec = lax.axis_index("section")
    nsec = lax.axis_size("section")
    pos_e = lax.axis_index("expert")
    x = pos_e // NZ
    z = lax.rem(pos_e, NZ)
    half = z // GROUP

    def dev(dx, dz, ds=0):
        xx = lax.rem(x + dx + NX, NX)
        zz = lax.rem(z + dz + NZ, NZ)
        return (lax.rem(sec + ds + nsec, nsec), xx * NZ + zz)

    def remote(src, dst, ss, rs, device):
        return pltpu.make_async_remote_copy(
            src_ref=src, dst_ref=dst, send_sem=ss, recv_sem=rs, device_id=device, device_id_type=MESH
        )

    barrier = pltpu.get_barrier_semaphore()
    partners = [dev(0, 1), dev(0, -1), dev(1, 0), dev(2, 0), dev(3, 0), dev(0, 0, 1), dev(0, 0, -1)]
    for partner in partners:
        pl.semaphore_signal(barrier, inc=1, device_id=partner, device_id_type=MESH)

    loads = [
        pltpu.make_async_copy(wg_ref, wgu.at[:, pl.ds(0, FF)], wsem.at[0]),
        pltpu.make_async_copy(wu_ref, wgu.at[:, pl.ds(FF, FF)], wsem.at[1]),
        pltpu.make_async_copy(wd_ref, wdv, wsem.at[2]),
    ]
    for load in loads:
        load.start()

    lane16 = lax.broadcasted_iota(jnp.int32, (TOK, LANES), 1)
    chosen = (lane16 == bid_ref[:, 0:1]) | (lane16 == bid_ref[:, 1:2])
    chosen = chosen | (lane16 == fid_ref[:, 0:1] + EF) | (lane16 == fid_ref[:, 1:2] + EF)
    zm[0] = jnp.where(chosen, 1.0, 0.0).astype(BF16)

    def normalize(v):
        wide = v.astype(F32)
        inv = lax.rsqrt(jnp.sum(wide * wide, axis=-1, keepdims=True) * (1.0 / D) + EPS)
        return wide, inv, (wide * inv).astype(BF16)

    _, _, hb = normalize(bx_ref[...])
    for c in range(NC):
        zb[0, c, 0] = hb[:, c * DC : (c + 1) * DC]
        zb[1, c, 0] = dy_ref[:, c * DC : (c + 1) * DC]

    pl.semaphore_wait(barrier, len(partners))

    def z_copy(a, c, slot):
        src = 0 if slot <= 2 else slot - 2
        target = dev(0, 1) if slot % 2 == 1 else dev(0, -1)
        if a < 0:
            return remote(zm.at[src], zm.at[slot], zms.at[slot - 1], zmr.at[slot - 1], target)
        return remote(zb.at[a, c, src], zb.at[a, c, slot], zs.at[a, c, slot - 1], zr.at[a, c, slot - 1], target)

    def pieces(a):
        return [(-1, 0), (0, 0), (0, 1)] if a == 0 else [(a, c) for c in range(NC)]

    def z_start(a):
        for piece in pieces(a):
            for slot in (1, 2):
                z_copy(*piece, slot).start()

    def z_step(a, k):
        for piece in pieces(a):
            for slot in (2 * k - 1, 2 * k):
                if slot < NZ:
                    z_copy(*piece, slot).wait_recv()
                    if slot + 2 < NZ:
                        z_copy(*piece, slot + 2).start()

    z_start(0)
    shift = remote(fx_ref, rx, shs, shr, dev(0, 0, 1))
    shift.start()

    cpad[...] = jnp.zeros_like(cpad)
    cpad[pl.ds(0, 2 * EF), :] = jnp.concatenate([cent_ref[...], cent_ref[...]], axis=0)
    for st in range(2 * NC):
        for gam in range(2):
            yr[st, gam, pl.ds(ROWS, 256 - ROWS), :] = jnp.zeros((256 - ROWS, DC), BF16)
    for gam in range(2):
        ypr[gam, pl.ds(ROWS, 256 - ROWS), :] = jnp.zeros((256 - ROWS, LANES), BF16)

    lane = lax.broadcasted_iota(jnp.int32, (GT, LANES), 1)

    def table(ab, gam):
        mask = zm[pl.ds(GROUP * gam, GROUP)].reshape(GT, LANES)
        row_i = lax.broadcasted_iota(jnp.int32, (GT, GT), 0)
        col_i = lax.broadcasted_iota(jnp.int32, (GT, GT), 1)
        below = jnp.where((row_i // TOK == col_i // TOK) & (col_i < row_i), 1.0, 0.0).astype(BF16)
        place = dot(below, mask)
        maskf = mask.astype(F32)
        base = (lax.broadcasted_iota(jnp.int32, (GT, 1), 0) // TOK * CAP).astype(F32)
        wide_lane = lax.broadcasted_iota(jnp.int32, (GT, 256), 1).astype(F32)
        total = jnp.zeros((GT, 256), F32)
        for d in range(NX):
            expert = 2 * lax.rem(x + d, NX) + half + EF * ab
            pick = lane == expert
            named = jnp.sum(jnp.where(pick, maskf, 0.0), axis=1, keepdims=True)
            slot = jnp.sum(jnp.where(pick, place, 0.0), axis=1, keepdims=True) + base + float(SLOTS * d)
            total = total + jnp.where(wide_lane == slot, named, 0.0)
        tu[ab, gam] = total.astype(BF16)
        tt[ab, gam] = total.T[:ROWS].astype(BF16)

    def gates_of(logits, mask, ab, width):
        inside = (width >= EF * ab) & (width < EF * (ab + 1)) & (mask > 0)
        aff = sigmoid(logits)
        picked = jnp.where(inside, aff, 0.0)
        denom = jnp.sum(picked, axis=1, keepdims=True)
        return inside, aff, denom, picked / denom

    def gates(ab, gam):
        a = 2 * ab
        acc = jnp.zeros((GT, LANES), F32)
        for c in range(NC):
            def add(k, acc, c=c):
                col = pl.multiple_of(k * STEP, STEP)
                rows = zb[a, c, pl.ds(GROUP * gam, GROUP), :, pl.ds(col, STEP)].reshape(GT, STEP)
                return acc + dot_nt(rows, cpad[:, pl.ds(c * DC + col, STEP)])
            acc = lax.fori_loop(0, DC // STEP, add, acc)
        mask = zm[pl.ds(GROUP * gam, GROUP)].reshape(GT, LANES).astype(F32)
        _, _, _, share = gates_of(acc, mask, ab, lane)
        block = lax.broadcasted_iota(jnp.int32, (GT, 256), 1) // SLOTS
        spread = jnp.zeros((GT, 256), F32)
        for d in range(NX):
            expert = 2 * lax.rem(x + d, NX) + half + EF * ab
            g = jnp.sum(jnp.where(lane == expert, share, 0.0), axis=1, keepdims=True)
            spread = jnp.where(block == d, g, spread)
        full = tu[ab, gam].astype(F32) * spread
        high = full.astype(BF16)
        thi[ab, gam] = high
        tlo[ab, gam] = (full - high.astype(F32)).astype(BF16)

    def x_copy(a, gam, d):
        return remote(
            xs.at[a, gam, d - 1], xr.at[a, gam, d], xss.at[a, gam, d - 1], xrs.at[a, gam, d - 1], dev(d, 0)
        )

    def select(a, gam):
        ab = a // 2
        for c in range(NC):
            @pl.loop(0, DC // STEP)
            def _(n, c=c):
                col = pl.multiple_of(n * STEP, STEP)
                rows = zb[a, c, pl.ds(GROUP * gam, GROUP), :, pl.ds(col, STEP)].reshape(GT, STEP)
                got = dot(tt[ab, gam], rows).astype(BF16)
                out = pl.ds(c * DC + col, STEP)
                xr[a, gam, 0, :, out] = got[:SLOTS]
                for d in range(1, NX):
                    xs[a, gam, d - 1, :, out] = got[SLOTS * d : SLOTS * (d + 1)]
        for d in (2, 1, 3):
            x_copy(a, gam, d).start()

    def x_wait(a, gam):
        for d in range(1, NX):
            x_copy(a, gam, d).wait_recv()

    def products(a, gam):
        def add(k, acc):
            cols = pl.ds(pl.multiple_of(k * DEPTH, DEPTH), DEPTH)
            return acc + dot(xr[a, gam, :, :, cols].reshape(ROWS, DEPTH), wgu[cols, :])
        return lax.fori_loop(0, D // DEPTH, add, jnp.zeros((ROWS, 2 * FF), F32))

    def y_copy(st, gam, d):
        return remote(
            ys.at[st, gam, d - 1], yr.at[st, gam, pl.ds(SLOTS * d, SLOTS)],
            yss.at[st, gam, d - 1], yrs.at[st, gam, d - 1], dev(-d, 0),
        )

    def yp_copy(gam, d):
        return remote(
            yps.at[gam, d - 1], ypr.at[gam, pl.ds(SLOTS * d, SLOTS)],
            ypss.at[gam, d - 1], yprs.at[gam, d - 1], dev(-d, 0),
        )

    def send_back(ab, gam, left, product):
        for c in range(NC):
            st = NC * ab + c
            @pl.loop(0, DC // STEP)
            def _(n, c=c, st=st):
                col = pl.multiple_of(n * STEP, STEP)
                got = product(left, pl.ds(c * DC + col, STEP)).astype(BF16)
                yr[st, gam, pl.ds(0, SLOTS), pl.ds(col, STEP)] = got[:SLOTS]
                for d in range(1, NX):
                    ys[st, gam, d - 1, :, pl.ds(col, STEP)] = got[SLOTS * d : SLOTS * (d + 1)]
            for d in (2, 1, 3):
                y_copy(st, gam, d).start()

    def expert_backward(gam):
        uv = uvb[gam]
        u, v = uv[:, :FF], uv[:, FF:]
        def add(k, acc):
            cols = pl.ds(pl.multiple_of(k * DEPTH, DEPTH), DEPTH)
            return acc + dot_nt(xr[1, gam, :, :, cols].reshape(ROWS, DEPTH), wdv[:, cols])
        q = lax.fori_loop(0, D // DEPTH, add, jnp.zeros((ROWS, FF), F32))
        sig = sigmoid(u)
        act = (u * sig * v).astype(BF16)
        p = jnp.sum(act.astype(F32) * q, axis=1, keepdims=True)
        du = (q * v * sig * (1.0 + u * (1.0 - sig))).astype(BF16)
        dv = (q * u * sig).astype(BF16)
        own = lax.broadcasted_iota(jnp.int32, (ROWS, LANES), 1) == 2 * x + half
        pw = jnp.where(own, p, 0.0).astype(BF16)
        ypr[gam, pl.ds(0, SLOTS), :] = pw[:SLOTS]
        for d in range(1, NX):
            yps[gam, d - 1] = pw[SLOTS * d : SLOTS * (d + 1)]
            yp_copy(gam, d).start()
        send_back(0, gam, jnp.concatenate([du, dv], axis=1), lambda left, cols: dot_nt(left, wgu[cols, :]))

    def expert_forward(gam):
        uv = products(2, gam)
        u, v = uv[:, :FF], uv[:, FF:]
        act = (u * sigmoid(u) * v).astype(BF16)
        send_back(1, gam, act, lambda left, cols: dot(left, wdv[:, cols]))

    def combine(ab, gam):
        for c in range(NC):
            st = NC * ab + c
            for d in range(1, NX):
                y_copy(st, gam, d).wait_recv()
            @pl.loop(0, DC // STEP)
            def _(n, st=st):
                cols = pl.ds(pl.multiple_of(n * STEP, STEP), STEP)
                rows = yr[st, gam, :, cols]
                part = dot(thi[ab, gam], rows) + dot(tlo[ab, gam], rows)
                pacc[st, pl.ds(GROUP * gam, GROUP), :, cols] = part.reshape(GROUP, TOK, STEP)
        if ab == 0:
            for d in range(1, NX):
                yp_copy(gam, d).wait_recv()
            pp[pl.ds(GROUP * gam, GROUP)] = dot(tu[0, gam], ypr[gam]).reshape(GROUP, TOK, LANES)

    def ring_copy(st, slot):
        i = slot - 1
        target = dev(0, -1) if slot % 2 == 1 else dev(0, 1)
        if st < 0:
            return remote(rps.at[i], rpr.at[i], rpss.at[i], rprs.at[i], target)
        return remote(rss.at[st, i], rsr.at[st, i], rsss.at[st, i], rsrs.at[st, i], target)

    def ring_sum(streams, slots):
        for slot in slots:
            for st in streams:
                val = pp[slot] if st < 0 else pacc[st, slot]
                if slot + 2 < NZ:
                    ring_copy(st, slot + 2).wait_recv()
                    val = val + (rpr[slot + 1] if st < 0 else rsr[st, slot + 1]).astype(F32)
                if st < 0:
                    rps[slot - 1] = val.astype(BF16)
                else:
                    rss[st, slot - 1] = val.astype(BF16)
                ring_copy(st, slot).start()

    def ring_result(st):
        for slot in (1, 2):
            ring_copy(st, slot).wait_recv()
        if st < 0:
            return pp[0] + rpr[0].astype(F32) + rpr[1].astype(F32)
        return pacc[st, 0] + rsr[st, 0].astype(F32) + rsr[st, 1].astype(F32)

    for k in range(1, 5):
        z_step(0, k)
    table(0, 0)
    select(0, 0)
    for k in range(5, 9):
        z_step(0, k)
        if k == 6:
            z_start(1)
    table(0, 1)
    select(0, 1)
    for k in range(1, 5):
        z_step(1, k)
    select(1, 0)
    table(1, 0)
    table(1, 1)
    shift.wait_recv()
    _, _, hf = normalize(rx[...])
    for c in range(NC):
        zb[2, c, 0] = hf[:, c * DC : (c + 1) * DC]
    for k in range(5, 9):
        z_step(1, k)
        if k == 6:
            z_start(2)
    select(1, 1)
    for k in range(1, 5):
        z_step(2, k)
    select(2, 0)
    for k in range(5, 9):
        z_step(2, k)
    select(2, 1)

    for load in loads:
        load.wait()
    for gam in range(2):
        gates(0, gam)
        gates(1, gam)
    for gam in range(2):
        x_wait(0, gam)
        uvb[gam] = products(0, gam)
    for gam in range(2):
        x_wait(1, gam)
        expert_backward(gam)
    for gam in range(2):
        x_wait(2, gam)
        expert_forward(gam)

    back = [0, 1, -1]
    combine(0, 1)
    ring_sum(back, range(15, 7, -1))
    combine(0, 0)
    ring_sum(back, range(7, 0, -1))
    dots = ring_result(-1)
    xb, rb, hown = normalize(bx_ref[...])
    mask0 = zm[0].astype(F32)
    logits = dot_nt(hown, cpad[...])
    inside, aff, denom, share = gates_of(logits, mask0, 0, lane16)
    scaled = ROUTE_SCALE * dots
    centre = jnp.sum(jnp.where(inside, share * scaled, 0.0), axis=1, keepdims=True)
    slope = jnp.where(inside, (scaled - centre) / denom * aff * (1.0 - aff), 0.0)
    s1 = slope.astype(BF16)
    s2f = slope - s1.astype(F32)
    s2 = s2f.astype(BF16)
    s3 = (s2f - s2.astype(F32)).astype(BF16)
    dh = jnp.concatenate([ring_result(0), ring_result(1)], axis=1) * ROUTE_SCALE
    dh = dh + dot(s1, cpad[...]) + (dot(s2, cpad[...]) + dot(s3, cpad[...]))
    proj = jnp.sum(dh * xb, axis=1, keepdims=True) * (1.0 / D)
    outb_ref[...] = (dy_ref[...].astype(F32) + rb * dh - rb * rb * rb * xb * proj).astype(BF16)

    front = [2, 3]
    combine(1, 1)
    ring_sum(front, range(15, 7, -1))
    combine(1, 0)
    ring_sum(front, range(7, 0, -1))
    for c in range(NC):
        cols = pl.ds(c * DC, DC)
        outf_ref[:, cols] = (rx[:, cols].astype(F32) + ROUTE_SCALE * ring_result(NC + c)).astype(BF16)

    shift.wait_send()
    for slot in range(1, NZ):
        for a in range(3):
            for piece in pieces(a):
                z_copy(*piece, slot).wait_send()
        for st in range(-1, 2 * NC):
            ring_copy(st, slot).wait_send()
    for gam in range(2):
        for d in range(1, NX):
            for a in range(3):
                x_copy(a, gam, d).wait_send()
            for st in range(2 * NC):
                y_copy(st, gam, d).wait_send()
            yp_copy(gam, d).wait_send()


def on_device(fwd_input, fwd_ids, bwd_input, bwd_ids, bwd_cot, centroids, w_gate, w_up, w_down):
    D = fwd_input.shape[-1]
    DC = D // NC
    FF = w_gate.shape[-1]
    vmem = pl.BlockSpec(memory_space=pltpu.VMEM)
    anym = pl.BlockSpec(memory_space=pl.ANY)
    DMA = pltpu.SemaphoreType.DMA
    V = pltpu.VMEM
    outs = pl.pallas_call(
        kernel,
        out_shape=[jax.ShapeDtypeStruct((TOK, D), BF16)] * 2,
        in_specs=[vmem] * 6 + [anym] * 3,
        out_specs=[vmem] * 2,
        scratch_shapes=[
            V((D, 2 * FF), BF16),
            V((FF, D), BF16),
            V((LANES, D), BF16),
            V((TOK, D), BF16),
            V((NZ, TOK, LANES), BF16),
            V((3, NC, NZ, TOK, DC), BF16),
            V((2, 2, ROWS, GT), BF16),
            V((2, 2, GT, 256), BF16),
            V((2, 2, GT, 256), BF16),
            V((2, 2, GT, 256), BF16),
            V((3, 2, NX - 1, SLOTS, D), BF16),
            V((3, 2, NX, SLOTS, D), BF16),
            V((2 * NC, 2, 256, DC), BF16),
            V((2 * NC, 2, NX - 1, SLOTS, DC), BF16),
            V((2, 256, LANES), BF16),
            V((2, NX - 1, SLOTS, LANES), BF16),
            V((2 * NC, NZ, TOK, DC), F32),
            V((NZ, TOK, LANES), F32),
            V((2 * NC, NZ - 1, TOK, DC), BF16),
            V((2 * NC, NZ - 1, TOK, DC), BF16),
            V((NZ - 1, TOK, LANES), BF16),
            V((NZ - 1, TOK, LANES), BF16),
            V((2, ROWS, 2 * FF), F32),
            DMA((3,)),
            DMA,
            DMA,
            DMA((NZ - 1,)),
            DMA((NZ - 1,)),
            DMA((3, NC, NZ - 1)),
            DMA((3, NC, NZ - 1)),
            DMA((3, 2, NX - 1)),
            DMA((3, 2, NX - 1)),
            DMA((2 * NC, 2, NX - 1)),
            DMA((2 * NC, 2, NX - 1)),
            DMA((2, NX - 1)),
            DMA((2, NX - 1)),
            DMA((2 * NC, NZ - 1)),
            DMA((2 * NC, NZ - 1)),
            DMA((NZ - 1,)),
            DMA((NZ - 1,)),
        ],
        compiler_params=pltpu.CompilerParams(
            collective_id=0, has_side_effects=True, vmem_limit_bytes=60 * 2**20
        ),
        cost_estimate=pl.CostEstimate(flops=6 * 10**9, bytes_accessed=4 * 10**6, transcendentals=0),
        name="expert_layer",
    )(
        fwd_input[0], fwd_ids[0], bwd_input[0], bwd_ids[0], bwd_cot[0], centroids[0],
        w_gate[0], w_up[0], w_down[0],
    )
    return outs[0][None], outs[1][None]


def solution(mesh):
    return jax.shard_map(
        on_device,
        mesh=mesh,
        in_specs=(
            P("section", "expert", None),
            P("section", "expert", None),
            P("section", "expert", None),
            P("section", "expert", None),
            P("section", "expert", None),
            P("section", None, None),
            P("section", None, "expert"),
            P("section", None, "expert"),
            P("section", "expert", None),
        ),
        out_specs=(P("section", "expert", None), P("section", "expert", None)),
        check_vma=False,
    )
```

```python
import functools

import jax
import jax.numpy as jnp
from jax import lax
from jax.experimental import pallas as pl
from jax.experimental.pallas import tpu as pltpu
from jax.sharding import PartitionSpec as P

MESH = pl.DeviceIdType.MESH
EF = 8
CAP = 6
NX = 4
NZ = 16
TOK = 16
EPS = 1e-06
ROUTE_SCALE = 2.5
NC = 2
GROUP = NZ // 2
SLOTS = GROUP * CAP
ROWS = NX * SLOTS
GT = GROUP * TOK
LANES = 128
STEP = 256
F32 = jnp.float32
BF16 = jnp.bfloat16
NT = (((1,), (1,)), ((), ()))


def dot(a, b):
    return jnp.dot(a, b, preferred_element_type=F32)


def dot_nt(a, b):
    return lax.dot_general(a, b, NT, preferred_element_type=F32)


def sigmoid(v):
    return jax.nn.sigmoid(v)


def kernel(
    fx_ref, fid_ref, bx_ref, bid_ref, dy_ref, cent_ref, wg_ref, wu_ref, wd_ref,
    outf_ref, outb_ref,
    wgu, wdv, cpad, rx, zm, zb, tt, tu, thi, tlo, xs, xr, xps, xpr, yr, ys, ypart, ymate, ysum, ypr2, ypr, yps,
    pacc, pp, rss, rsr, rps, rpr, uvb,
    wsem, shs, shr, zms, zmr, zs, zr, xss, xrs, xpss, xprs, rls, rlr, yss, yrs, yms, ymr, yus, yur, ypss, yprs,
    rsss, rsrs, rpss, rprs,
):
    D = fx_ref.shape[-1]
    DC = D // NC
    W = DC // 2
    FF = wdv.shape[0]
    sec = lax.axis_index("section")
    nsec = lax.axis_size("section")
    pos_e = lax.axis_index("expert")
    x = pos_e // NZ
    z = lax.rem(pos_e, NZ)
    half = z // GROUP
    par = lax.rem(z, 2)
    mate_step = 1 - 2 * par

    def dev(dx, dz, ds=0):
        xx = lax.rem(x + dx + NX, NX)
        zz = lax.rem(z + dz + NZ, NZ)
        return (lax.rem(sec + ds + nsec, nsec), xx * NZ + zz)

    def remote(src, dst, ss, rs, device):
        return pltpu.make_async_remote_copy(
            src_ref=src, dst_ref=dst, send_sem=ss, recv_sem=rs, device_id=device, device_id_type=MESH
        )

    barrier = pltpu.get_barrier_semaphore()
    partners = [dev(0, 1), dev(0, -1), dev(1, 0), dev(2, 0), dev(3, 0), dev(0, 0, 1), dev(0, 0, -1)]
    for partner in partners:
        pl.semaphore_signal(barrier, inc=1, device_id=partner, device_id_type=MESH)

    loads = [
        pltpu.make_async_copy(wg_ref, wgu.at[:, pl.ds(0, FF)], wsem.at[0]),
        pltpu.make_async_copy(wu_ref, wgu.at[:, pl.ds(FF, FF)], wsem.at[1]),
        pltpu.make_async_copy(wd_ref, wdv, wsem.at[2]),
    ]
    for load in loads:
        load.start()

    lane16 = lax.broadcasted_iota(jnp.int32, (TOK, LANES), 1)
    chosen = (lane16 == bid_ref[:, 0:1]) | (lane16 == bid_ref[:, 1:2])
    chosen = chosen | (lane16 == fid_ref[:, 0:1] + EF) | (lane16 == fid_ref[:, 1:2] + EF)
    zm[0] = jnp.where(chosen, 1.0, 0.0).astype(BF16)

    def normalize(v):
        wide = v.astype(F32)
        inv = lax.rsqrt(jnp.sum(wide * wide, axis=-1, keepdims=True) * (1.0 / D) + EPS)
        return wide, inv, (wide * inv).astype(BF16)

    _, _, hb = normalize(bx_ref[...])
    for c in range(NC):
        zb[0, c, 0] = hb[:, c * DC : (c + 1) * DC]
        zb[1, c, 0] = dy_ref[:, c * DC : (c + 1) * DC]

    pl.semaphore_wait(barrier, len(partners))

    def place_of(slot, parity):
        return 8 - parity if slot == 7 else 7 + parity if slot == 8 else slot

    def z_copy(a, c, slot):
        src = 0 if slot <= 2 else place_of(slot - 2, par)
        dst = place_of(slot, 1 - par)
        target = dev(0, 1) if slot % 2 == 1 else dev(0, -1)
        if a < 0:
            return remote(zm.at[src], zm.at[dst], zms.at[slot - 1], zmr.at[slot - 1], target)
        return remote(zb.at[a, c, src], zb.at[a, c, dst], zs.at[a, c, slot - 1], zr.at[a, c, slot - 1], target)

    def pieces(a):
        return [(-1, 0), (0, 0), (0, 1)] if a == 0 else [(a, c) for c in range(NC)]

    def z_start(a):
        for piece in pieces(a):
            for slot in (1, 2):
                z_copy(*piece, slot).start()

    def z_step(a, k):
        for piece in pieces(a):
            for slot in (2 * k - 1, 2 * k):
                if slot < NZ:
                    z_copy(*piece, slot).wait_recv()
                    if slot + 2 < NZ:
                        z_copy(*piece, slot + 2).start()

    z_start(0)
    shift = remote(fx_ref, rx, shs, shr, dev(0, 0, 1))
    shift.start()

    cpad[...] = jnp.zeros_like(cpad)
    cpad[pl.ds(0, 2 * EF), :] = jnp.concatenate([cent_ref[...], cent_ref[...]], axis=0)
    for ab in range(2):
        for gam in range(2):
            yr[ab, gam, pl.ds(ROWS, 256 - ROWS), :] = jnp.zeros((256 - ROWS, DC), BF16)
            ypr2[ab, gam, par, pl.ds(ROWS, 256 - ROWS), :] = jnp.zeros((256 - ROWS, W), BF16)
            ypr2[ab, gam, 1 - par, pl.ds(SLOTS, 256 - SLOTS), :] = jnp.zeros((256 - SLOTS, W), BF16)
    for gam in range(2):
        ypr[gam, pl.ds(ROWS, 256 - ROWS), :] = jnp.zeros((256 - ROWS, LANES), BF16)

    lane = lax.broadcasted_iota(jnp.int32, (GT, LANES), 1)

    def away(place, parity):
        if place in (7, 8):
            return -4 if (place == 7) == (parity == 1) else 4
        return place // 2 if place % 2 == 0 else -(place + 1) // 2

    def table(ab, gam):
        mask = zm[pl.ds(GROUP * gam, GROUP)].reshape(GT, LANES)
        row_i = lax.broadcasted_iota(jnp.int32, (GT, GT), 0)
        col_i = lax.broadcasted_iota(jnp.int32, (GT, GT), 1)
        below = jnp.where((row_i // TOK == col_i // TOK) & (col_i < row_i), 1.0, 0.0).astype(BF16)
        place = dot(below, mask)
        maskf = mask.astype(F32)
        block = lax.broadcasted_iota(jnp.int32, (GT, 1), 0) // TOK
        order = jnp.zeros((GT, 1), jnp.int32)
        for b in range(GROUP):
            even, odd = [(away(b + GROUP * gam, parity) + parity + 3 - GROUP * gam) % NZ for parity in (0, 1)]
            order = jnp.where(block == b, even + (odd - even) * par, order)
        base = (order * CAP).astype(F32)
        wide_lane = lax.broadcasted_iota(jnp.int32, (GT, 256), 1).astype(F32)
        total = jnp.zeros((GT, 256), F32)
        for d in range(NX):
            expert = 2 * lax.rem(x + d, NX) + half + EF * ab
            pick = lane == expert
            named = jnp.sum(jnp.where(pick, maskf, 0.0), axis=1, keepdims=True)
            slot = jnp.sum(jnp.where(pick, place, 0.0), axis=1, keepdims=True) + base + float(SLOTS * d)
            total = total + jnp.where(wide_lane == slot, named, 0.0)
        tu[ab, gam] = total.astype(BF16)
        tt[ab, gam] = total.T[:ROWS].astype(BF16)

    def gates_of(logits, mask, ab, width):
        inside = (width >= EF * ab) & (width < EF * (ab + 1)) & (mask > 0)
        aff = sigmoid(logits)
        picked = jnp.where(inside, aff, 0.0)
        denom = jnp.sum(picked, axis=1, keepdims=True)
        return inside, aff, denom, picked / denom

    def gates(ab, gam):
        a = 2 * ab
        acc = jnp.zeros((GT, LANES), F32)
        for c in range(NC):
            def add(k, acc, c=c):
                col = pl.multiple_of(k * STEP, STEP)
                rows = zb[a, c, pl.ds(GROUP * gam, GROUP), :, pl.ds(col, STEP)].reshape(GT, STEP)
                return acc + dot_nt(rows, cpad[:, pl.ds(c * DC + col, STEP)])
            acc = lax.fori_loop(0, DC // STEP, add, acc)
        mask = zm[pl.ds(GROUP * gam, GROUP)].reshape(GT, LANES).astype(F32)
        _, _, _, share = gates_of(acc, mask, ab, lane)
        block = lax.broadcasted_iota(jnp.int32, (GT, 256), 1) // SLOTS
        spread = jnp.zeros((GT, 256), F32)
        for d in range(NX):
            expert = 2 * lax.rem(x + d, NX) + half + EF * ab
            g = jnp.sum(jnp.where(lane == expert, share, 0.0), axis=1, keepdims=True)
            spread = jnp.where(block == d, g, spread)
        full = tu[ab, gam].astype(F32) * spread
        high = full.astype(BF16)
        thi[ab, gam] = high
        tlo[ab, gam] = (full - high.astype(F32)).astype(BF16)

    def x_copy(a, gam, d):
        return remote(
            xs.at[a, gam, d - 1], xr.at[a, gam, d], xss.at[a, gam, d - 1], xrs.at[a, gam, d - 1], dev(d, 0)
        )

    def xp_copy(a, gam, d):
        return remote(
            xps.at[a, gam, d - 1], xpr.at[a, gam, par, d], xpss.at[a, gam, d - 1], xprs.at[a, gam, d - 1], dev(d, 0)
        )

    def relay_copy(a, gam):
        part = xpr.at[a, gam, par, pl.ds(1, NX - 1)]
        return remote(part, part, rls.at[a, gam], rlr.at[a, gam], dev(0, mate_step))

    def tokens(a, c, gam, cols):
        return zb[a, c, pl.ds(GROUP * gam, GROUP), :, cols].reshape(GT, -1)

    def select(a, gam, before=None):
        ab = a // 2
        got = dot(tt[ab, gam, pl.ds(SLOTS, ROWS - SLOTS), :],
                  tokens(a, 0, gam, pl.ds(pl.multiple_of(par * W, LANES), W))).astype(BF16)
        for d in range(1, NX):
            xps[a, gam, d - 1] = got[SLOTS * (d - 1) : SLOTS * d]
        if before is not None:
            x_sent(*before)
        for d in (2, 1, 3):
            xp_copy(a, gam, d).start()
        for h in range(2):
            cols = pl.ds(h * W, W)
            got = dot(tt[ab, gam], tokens(a, 1, gam, cols)).astype(BF16)
            xr[a, gam, 0, :, cols] = got[:SLOTS]
            for d in range(1, NX):
                xs[a, gam, d - 1, :, cols] = got[SLOTS * d : SLOTS * (d + 1)]
        for d in (2, 1, 3):
            x_copy(a, gam, d).start()
        for h in range(2):
            got = dot(tt[ab, gam, pl.ds(0, SLOTS), :], tokens(a, 0, gam, pl.ds(h * W, W)))
            xpr[a, gam, h, 0] = got.astype(BF16)

    def x_sent(a, gam):
        for d in range(1, NX):
            xp_copy(a, gam, d).wait_send()
            x_copy(a, gam, d).wait_send()

    def relay(a, gam):
        for d in range(1, NX):
            xp_copy(a, gam, d).wait_recv()
        relay_copy(a, gam).start()

    def x_wait(a, gam):
        for d in range(1, NX):
            x_copy(a, gam, d).wait_recv()
        relay_copy(a, gam).wait_recv()

    def rows_of(a, gam, j):
        if j < 2:
            return xpr[a, gam, j].reshape(ROWS, W)
        return xr[a, gam, :, :, pl.ds((j - 2) * W, W)].reshape(ROWS, W)

    def products(a, gam):
        acc = jnp.zeros((ROWS, 2 * FF), F32)
        for j in range(4):
            acc = acc + dot(rows_of(a, gam, j), wgu[pl.ds(j * W, W), :])
        return acc

    def y_copy(ab, gam, d):
        return remote(
            ys.at[ab, gam, d - 1], yr.at[ab, gam, pl.ds(SLOTS * d, SLOTS)],
            yss.at[ab, gam, d - 1], yrs.at[ab, gam, d - 1], dev(-d, 0),
        )

    def mate_copy(ab, gam):
        return remote(
            ypart.at[ab, gam, 1 - par], ymate.at[ab, gam], yms.at[ab, gam], ymr.at[ab, gam], dev(0, mate_step)
        )

    def ysum_copy(ab, gam, d):
        return remote(
            ysum.at[ab, gam, d - 1], ypr2.at[ab, gam, par, pl.ds(SLOTS * d, SLOTS)],
            yus.at[ab, gam, d - 1], yur.at[ab, gam, d - 1], dev(-d, 0),
        )

    def yp_copy(gam, d):
        return remote(
            yps.at[gam, d - 1], ypr.at[gam, pl.ds(SLOTS * d, SLOTS)],
            ypss.at[gam, d - 1], yprs.at[gam, d - 1], dev(-d, 0),
        )

    def send_back(ab, gam, left, product):
        for j in range(4):
            got = product(left, pl.ds(j * W, W)).astype(BF16)
            if j < 2:
                ypr2[ab, gam, j, pl.ds(0, SLOTS), :] = got[:SLOTS]
                for d in range(1, NX):
                    ypart[ab, gam, j, d - 1] = got[SLOTS * d : SLOTS * (d + 1)]
                if j == 1:
                    mate_copy(ab, gam).start()
            else:
                cols = pl.ds((j - 2) * W, W)
                yr[ab, gam, pl.ds(0, SLOTS), cols] = got[:SLOTS]
                for d in range(1, NX):
                    ys[ab, gam, d - 1, :, cols] = got[SLOTS * d : SLOTS * (d + 1)]

    def y_start(ab, gam):
        for d in (2, 1, 3):
            y_copy(ab, gam, d).start()

    def pair_start(ab, gam):
        mate_copy(ab, gam).wait_recv()
        for d in (2, 1, 3):
            both = ypart[ab, gam, par, d - 1].astype(F32) + ymate[ab, gam, d - 1].astype(F32)
            ysum[ab, gam, d - 1] = both.astype(BF16)
            ysum_copy(ab, gam, d).start()

    def y_sent(ab, gam):
        mate_copy(ab, gam).wait_send()
        for d in range(1, NX):
            y_copy(ab, gam, d).wait_send()
            ysum_copy(ab, gam, d).wait_send()

    def expert_backward(gam):
        uv = uvb[gam]
        u, v = uv[:, :FF], uv[:, FF:]
        q = jnp.zeros((ROWS, FF), F32)
        for j in range(4):
            q = q + dot_nt(rows_of(1, gam, j), wdv[:, pl.ds(j * W, W)])
        sig = sigmoid(u)
        act = (u * sig * v).astype(BF16)
        p = jnp.sum(act.astype(F32) * q, axis=1, keepdims=True)
        du = (q * v * sig * (1.0 + u * (1.0 - sig))).astype(BF16)
        dv = (q * u * sig).astype(BF16)
        own = lax.broadcasted_iota(jnp.int32, (ROWS, LANES), 1) == 2 * x + half
        pw = jnp.where(own, p, 0.0).astype(BF16)
        ypr[gam, pl.ds(0, SLOTS), :] = pw[:SLOTS]
        for d in range(1, NX):
            yps[gam, d - 1] = pw[SLOTS * d : SLOTS * (d + 1)]
            yp_copy(gam, d).start()
        send_back(0, gam, jnp.concatenate([du, dv], axis=1), lambda left, cols: dot_nt(left, wgu[cols, :]))

    def expert_forward(gam):
        uv = products(2, gam)
        u, v = uv[:, :FF], uv[:, FF:]
        act = (u * sigmoid(u) * v).astype(BF16)
        send_back(1, gam, act, lambda left, cols: dot(left, wdv[:, cols]))

    def combine(ab, gam):
        for d in range(1, NX):
            y_copy(ab, gam, d).wait_recv()
            ysum_copy(ab, gam, d).wait_recv()
        for j in range(4):
            cols = pl.ds((j % 2) * W, W)
            rows = ypr2[ab, gam, j] if j < 2 else yr[ab, gam, :, cols]
            part = dot(thi[ab, gam], rows) + dot(tlo[ab, gam], rows)
            pacc[NC * ab + j // 2, pl.ds(GROUP * gam, GROUP), :, cols] = part.reshape(GROUP, TOK, W)
        if ab == 0:
            for d in range(1, NX):
                yp_copy(gam, d).wait_recv()
            pp[pl.ds(GROUP * gam, GROUP)] = dot(tu[0, gam], ypr[gam]).reshape(GROUP, TOK, LANES)

    def ring_copy(st, slot):
        i = slot - 1
        target = dev(0, -1) if slot % 2 == 1 else dev(0, 1)
        if st < 0:
            return remote(rps.at[i], rpr.at[i], rpss.at[i], rprs.at[i], target)
        return remote(rss.at[st, i], rsr.at[st, i], rsss.at[st, i], rsrs.at[st, i], target)

    def ring_sum(streams, slots):
        for slot in slots:
            for st in streams:
                place = place_of(slot, par)
                val = pp[place] if st < 0 else pacc[st, place]
                if slot + 2 < NZ:
                    ring_copy(st, slot + 2).wait_recv()
                    val = val + (rpr[slot + 1] if st < 0 else rsr[st, slot + 1]).astype(F32)
                if st < 0:
                    rps[slot - 1] = val.astype(BF16)
                else:
                    rss[st, slot - 1] = val.astype(BF16)
                ring_copy(st, slot).start()

    def ring_result(st):
        for slot in (1, 2):
            ring_copy(st, slot).wait_recv()
        if st < 0:
            return pp[0] + rpr[0].astype(F32) + rpr[1].astype(F32)
        return pacc[st, 0] + rsr[st, 0].astype(F32) + rsr[st, 1].astype(F32)

    for k in range(1, 5):
        z_step(0, k)
    z_start(1)
    table(0, 0)
    select(0, 0)
    shift.wait_recv()
    _, _, hf = normalize(rx[...])
    for c in range(NC):
        zb[2, c, 0] = hf[:, c * DC : (c + 1) * DC]
    for k in range(1, 5):
        z_step(0, k + 4)
        z_step(1, k)
    z_start(2)
    table(0, 1)
    select(0, 1)
    select(1, 0)
    relay(0, 0)
    for k in range(1, 5):
        z_step(1, k + 4)
        z_step(2, k)
    table(1, 0)
    table(1, 1)
    select(1, 1)
    select(2, 0)
    relay(0, 1)
    relay(1, 0)
    for k in range(5, 9):
        z_step(2, k)
    select(2, 1)
    relay(1, 1)

    for load in loads:
        load.wait()
    for gam in (0, 1):
        gates(0, gam)
        x_wait(0, gam)
        uvb[gam] = products(0, gam)
    relay(2, 0)
    for gam in (1, 0):
        x_wait(1, gam)
        expert_backward(gam)
        y_start(0, gam)
    relay(2, 1)
    pair_start(0, 1)
    pair_start(0, 0)
    for gam in (1, 0):
        gates(1, gam)
        x_wait(2, gam)
        expert_forward(gam)
        y_start(1, gam)
    pair_start(1, 1)
    pair_start(1, 0)
    back = [0, 1, -1]
    front = [2, 3]
    combine(0, 1)
    ring_sum(back, range(15, 8, -1))
    combine(0, 0)
    combine(1, 1)
    for slot in range(7, 0, -1):
        ring_sum(back, [slot + 1])
        ring_sum(front, [slot + 8])
    ring_sum(back, [1])
    dots = ring_result(-1)
    xb, rb, hown = normalize(bx_ref[...])
    mask0 = zm[0].astype(F32)
    logits = dot_nt(hown, cpad[...])
    inside, aff, denom, share = gates_of(logits, mask0, 0, lane16)
    scaled = ROUTE_SCALE * dots
    centre = jnp.sum(jnp.where(inside, share * scaled, 0.0), axis=1, keepdims=True)
    slope = jnp.where(inside, (scaled - centre) / denom * aff * (1.0 - aff), 0.0)
    s1 = slope.astype(BF16)
    s2f = slope - s1.astype(F32)
    s2 = s2f.astype(BF16)
    s3 = (s2f - s2.astype(F32)).astype(BF16)
    dh = jnp.concatenate([ring_result(0), ring_result(1)], axis=1) * ROUTE_SCALE
    dh = dh + dot(s1, cpad[...]) + (dot(s2, cpad[...]) + dot(s3, cpad[...]))
    proj = jnp.sum(dh * xb, axis=1, keepdims=True) * (1.0 / D)
    outb_ref[...] = (dy_ref[...].astype(F32) + rb * dh - rb * rb * rb * xb * proj).astype(BF16)

    combine(1, 0)
    ring_sum(front, range(8, 0, -1))
    for c in range(NC):
        cols = pl.ds(c * DC, DC)
        outf_ref[:, cols] = (rx[:, cols].astype(F32) + ROUTE_SCALE * ring_result(NC + c)).astype(BF16)

    shift.wait_send()
    for slot in range(1, NZ):
        for a in range(3):
            for piece in pieces(a):
                z_copy(*piece, slot).wait_send()
        for st in range(-1, 2 * NC):
            ring_copy(st, slot).wait_send()
    for gam in range(2):
        for a in range(3):
            x_sent(a, gam)
            relay_copy(a, gam).wait_send()
        for ab in range(2):
            y_sent(ab, gam)
        for d in range(1, NX):
            yp_copy(gam, d).wait_send()


def on_device(fwd_input, fwd_ids, bwd_input, bwd_ids, bwd_cot, centroids, w_gate, w_up, w_down):
    D = fwd_input.shape[-1]
    DC = D // NC
    W = DC // 2
    FF = w_gate.shape[-1]
    vmem = pl.BlockSpec(memory_space=pltpu.VMEM)
    anym = pl.BlockSpec(memory_space=pl.ANY)
    DMA = pltpu.SemaphoreType.DMA
    V = pltpu.VMEM
    outs = pl.pallas_call(
        kernel,
        out_shape=[jax.ShapeDtypeStruct((TOK, D), BF16)] * 2,
        in_specs=[vmem] * 6 + [anym] * 3,
        out_specs=[vmem] * 2,
        scratch_shapes=[
            V((D, 2 * FF), BF16),
            V((FF, D), BF16),
            V((LANES, D), BF16),
            V((TOK, D), BF16),
            V((NZ, TOK, LANES), BF16),
            V((3, NC, NZ, TOK, DC), BF16),
            V((2, 2, ROWS, GT), BF16),
            V((2, 2, GT, 256), BF16),
            V((2, 2, GT, 256), BF16),
            V((2, 2, GT, 256), BF16),
            V((3, 2, NX - 1, SLOTS, DC), BF16),
            V((3, 2, NX, SLOTS, DC), BF16),
            V((3, 2, NX - 1, SLOTS, W), BF16),
            V((3, 2, 2, NX, SLOTS, W), BF16),
            V((2, 2, 256, DC), BF16),
            V((2, 2, NX - 1, SLOTS, DC), BF16),
            V((2, 2, 2, NX - 1, SLOTS, W), BF16),
            V((2, 2, NX - 1, SLOTS, W), BF16),
            V((2, 2, NX - 1, SLOTS, W), BF16),
            V((2, 2, 2, 256, W), BF16),
            V((2, 256, LANES), BF16),
            V((2, NX - 1, SLOTS, LANES), BF16),
            V((2 * NC, NZ, TOK, DC), F32),
            V((NZ, TOK, LANES), F32),
            V((2 * NC, NZ - 1, TOK, DC), BF16),
            V((2 * NC, NZ - 1, TOK, DC), BF16),
            V((NZ - 1, TOK, LANES), BF16),
            V((NZ - 1, TOK, LANES), BF16),
            V((2, ROWS, 2 * FF), F32),
            DMA((3,)),
            DMA,
            DMA,
            DMA((NZ - 1,)),
            DMA((NZ - 1,)),
            DMA((3, NC, NZ - 1)),
            DMA((3, NC, NZ - 1)),
            DMA((3, 2, NX - 1)),
            DMA((3, 2, NX - 1)),
            DMA((3, 2, NX - 1)),
            DMA((3, 2, NX - 1)),
            DMA((3, 2)),
            DMA((3, 2)),
            DMA((2, 2, NX - 1)),
            DMA((2, 2, NX - 1)),
            DMA((2, 2)),
            DMA((2, 2)),
            DMA((2, 2, NX - 1)),
            DMA((2, 2, NX - 1)),
            DMA((2, NX - 1)),
            DMA((2, NX - 1)),
            DMA((2 * NC, NZ - 1)),
            DMA((2 * NC, NZ - 1)),
            DMA((NZ - 1,)),
            DMA((NZ - 1,)),
        ],
        compiler_params=pltpu.CompilerParams(
            collective_id=0, has_side_effects=True, vmem_limit_bytes=60 * 2**20
        ),
        cost_estimate=pl.CostEstimate(flops=6 * 10**9, bytes_accessed=4 * 10**6, transcendentals=0),
        name="expert_layer",
    )(
        fwd_input[0], fwd_ids[0], bwd_input[0], bwd_ids[0], bwd_cot[0], centroids[0],
        w_gate[0], w_up[0], w_down[0],
    )
    return outs[0][None], outs[1][None]


def solution(mesh):
    return jax.shard_map(
        on_device,
        mesh=mesh,
        in_specs=(
            P("section", "expert", None),
            P("section", "expert", None),
            P("section", "expert", None),
            P("section", "expert", None),
            P("section", "expert", None),
            P("section", None, None),
            P("section", None, "expert"),
            P("section", None, "expert"),
            P("section", "expert", None),
        ),
        out_specs=(P("section", "expert", None), P("section", "expert", None)),
        check_vma=False,
    )
```

```python
import functools

import jax
import jax.numpy as jnp
from jax import lax
from jax.experimental import pallas as pl
from jax.experimental.pallas import tpu as pltpu
from jax.sharding import PartitionSpec as P

MESH = pl.DeviceIdType.MESH
EF = 8
CAP = 6
NX = 4
NZ = 16
TOK = 16
EPS = 1e-06
ROUTE_SCALE = 2.5
NC = 2
GROUP = NZ // 2
SLOTS = GROUP * CAP
ROWS = NX * SLOTS
GT = GROUP * TOK
LANES = 128
STEP = 256
F32 = jnp.float32
BF16 = jnp.bfloat16
NT = (((1,), (1,)), ((), ()))


def dot(a, b):
    return jnp.dot(a, b, preferred_element_type=F32)


def dot_nt(a, b):
    return lax.dot_general(a, b, NT, preferred_element_type=F32)


def sigmoid(v):
    return jax.nn.sigmoid(v)


def kernel(
    fx_ref, fid_ref, bx_ref, bid_ref, dy_ref, cent_ref, wg_ref, wu_ref, wd_ref,
    outf_ref, outb_ref,
    wgu, wdv, cpad, rx, zm, zb, tt, tu, thi, tlo, xs, xr, xps, xpr, yr, ys, ypart, ymate, ysum, ypr2, ypr, yps,
    pacc, rss, rsr, uvb, gsh, gco,
    wsem, shs, shr, zms, zmr, zs, zr, xss, xrs, xpss, xprs, rls, rlr, yss, yrs, yms, ymr, yus, yur, ypss, yprs,
    rsss, rsrs,
):
    D = fx_ref.shape[-1]
    DC = D // NC
    W = DC // 2
    FF = wdv.shape[0]
    sec = lax.axis_index("section")
    nsec = lax.axis_size("section")
    pos_e = lax.axis_index("expert")
    x = pos_e // NZ
    z = lax.rem(pos_e, NZ)
    half = z // GROUP
    par = lax.rem(z, 2)
    mate_step = 1 - 2 * par

    def dev(dx, dz, ds=0):
        xx = lax.rem(x + dx + NX, NX)
        zz = lax.rem(z + dz + NZ, NZ)
        return (lax.rem(sec + ds + nsec, nsec), xx * NZ + zz)

    def remote(src, dst, ss, rs, device):
        return pltpu.make_async_remote_copy(
            src_ref=src, dst_ref=dst, send_sem=ss, recv_sem=rs, device_id=device, device_id_type=MESH
        )

    barrier = pltpu.get_barrier_semaphore()
    partners = [dev(0, 1), dev(0, -1), dev(1, 0), dev(2, 0), dev(3, 0), dev(0, 0, 1), dev(0, 0, -1)]
    for partner in partners:
        pl.semaphore_signal(barrier, inc=1, device_id=partner, device_id_type=MESH)

    loads = [
        pltpu.make_async_copy(wg_ref, wgu.at[:, pl.ds(0, FF)], wsem.at[0]),
        pltpu.make_async_copy(wu_ref, wgu.at[:, pl.ds(FF, FF)], wsem.at[1]),
        pltpu.make_async_copy(wd_ref, wdv, wsem.at[2]),
    ]
    for load in loads:
        load.start()

    lane16 = lax.broadcasted_iota(jnp.int32, (TOK, LANES), 1)
    chosen = (lane16 == bid_ref[:, 0:1]) | (lane16 == bid_ref[:, 1:2])
    chosen = chosen | (lane16 == fid_ref[:, 0:1] + EF) | (lane16 == fid_ref[:, 1:2] + EF)
    zm[0] = jnp.where(chosen, 1.0, 0.0).astype(BF16)

    def normalize(v):
        wide = v.astype(F32)
        inv = lax.rsqrt(jnp.sum(wide * wide, axis=-1, keepdims=True) * (1.0 / D) + EPS)
        return wide, inv, (wide * inv).astype(BF16)

    _, _, hb = normalize(bx_ref[...])
    for c in range(NC):
        zb[0, c, 0] = hb[:, c * DC : (c + 1) * DC]
        zb[1, c, 0] = dy_ref[:, c * DC : (c + 1) * DC]

    pl.semaphore_wait(barrier, len(partners))

    def place_of(slot, parity):
        return 8 - parity if slot == 7 else 7 + parity if slot == 8 else slot

    def z_copy(a, c, slot):
        src = 0 if slot <= 2 else place_of(slot - 2, par)
        dst = place_of(slot, 1 - par)
        target = dev(0, 1) if slot % 2 == 1 else dev(0, -1)
        if a < 0:
            return remote(zm.at[src], zm.at[dst], zms.at[slot - 1], zmr.at[slot - 1], target)
        return remote(zb.at[a, c, src], zb.at[a, c, dst], zs.at[a, c, slot - 1], zr.at[a, c, slot - 1], target)

    def pieces(a):
        return [(-1, 0), (0, 0), (0, 1)] if a == 0 else [(a, c) for c in range(NC)]

    def z_start(a):
        for piece in pieces(a):
            for slot in (1, 2):
                z_copy(*piece, slot).start()

    def z_step(a, k):
        for piece in pieces(a):
            for slot in (2 * k - 1, 2 * k):
                if slot < NZ:
                    z_copy(*piece, slot).wait_recv()
                    if slot + 2 < NZ:
                        z_copy(*piece, slot + 2).start()

    z_start(0)
    shift = remote(fx_ref, rx, shs, shr, dev(0, 0, 1))
    shift.start()

    cpad[...] = jnp.zeros_like(cpad)
    cpad[pl.ds(0, 2 * EF), :] = jnp.concatenate([cent_ref[...], cent_ref[...]], axis=0)
    for ab in range(2):
        for gam in range(2):
            yr[ab, gam, pl.ds(ROWS, 256 - ROWS), :] = jnp.zeros((256 - ROWS, DC), BF16)
            ypr2[ab, gam, par, pl.ds(ROWS, 256 - ROWS), :] = jnp.zeros((256 - ROWS, W), BF16)
            ypr2[ab, gam, 1 - par, pl.ds(SLOTS, 256 - SLOTS), :] = jnp.zeros((256 - SLOTS, W), BF16)
    for gam in range(2):
        ypr[gam, pl.ds(ROWS, 256 - ROWS), :] = jnp.zeros((256 - ROWS, LANES), BF16)

    lane = lax.broadcasted_iota(jnp.int32, (GT, LANES), 1)

    def away(place, parity):
        if place in (7, 8):
            return -4 if (place == 7) == (parity == 1) else 4
        return place // 2 if place % 2 == 0 else -(place + 1) // 2

    def table(ab, gam):
        mask = zm[pl.ds(GROUP * gam, GROUP)].reshape(GT, LANES)
        row_i = lax.broadcasted_iota(jnp.int32, (GT, GT), 0)
        col_i = lax.broadcasted_iota(jnp.int32, (GT, GT), 1)
        below = jnp.where((row_i // TOK == col_i // TOK) & (col_i < row_i), 1.0, 0.0).astype(BF16)
        place = dot(below, mask)
        maskf = mask.astype(F32)
        block = lax.broadcasted_iota(jnp.int32, (GT, 1), 0) // TOK
        order = jnp.zeros((GT, 1), jnp.int32)
        for b in range(GROUP):
            even, odd = [(away(b + GROUP * gam, parity) + parity + 3 - GROUP * gam) % NZ for parity in (0, 1)]
            order = jnp.where(block == b, even + (odd - even) * par, order)
        base = (order * CAP).astype(F32)
        wide_lane = lax.broadcasted_iota(jnp.int32, (GT, 256), 1).astype(F32)
        total = jnp.zeros((GT, 256), F32)
        for d in range(NX):
            expert = 2 * lax.rem(x + d, NX) + half + EF * ab
            pick = lane == expert
            named = jnp.sum(jnp.where(pick, maskf, 0.0), axis=1, keepdims=True)
            slot = jnp.sum(jnp.where(pick, place, 0.0), axis=1, keepdims=True) + base + float(SLOTS * d)
            total = total + jnp.where(wide_lane == slot, named, 0.0)
        tu[ab, gam] = total.astype(BF16)
        tt[ab, gam] = total.T[:ROWS].astype(BF16)

    def gates_of(logits, mask, ab, width):
        inside = (width >= EF * ab) & (width < EF * (ab + 1)) & (mask > 0)
        aff = sigmoid(logits)
        picked = jnp.where(inside, aff, 0.0)
        denom = jnp.sum(picked, axis=1, keepdims=True)
        return inside, aff, denom, picked / denom

    def gates(ab, gam):
        a = 2 * ab
        acc = jnp.zeros((GT, LANES), F32)
        for c in range(NC):
            def add(k, acc, c=c):
                col = pl.multiple_of(k * STEP, STEP)
                rows = zb[a, c, pl.ds(GROUP * gam, GROUP), :, pl.ds(col, STEP)].reshape(GT, STEP)
                return acc + dot_nt(rows, cpad[:, pl.ds(c * DC + col, STEP)])
            acc = lax.fori_loop(0, DC // STEP, add, acc)
        mask = zm[pl.ds(GROUP * gam, GROUP)].reshape(GT, LANES).astype(F32)
        inside, aff, denom, share = gates_of(acc, mask, ab, lane)
        if ab == 0:
            gsh[gam] = share
            gco[gam] = jnp.where(inside, aff * (1.0 - aff) / denom, 0.0)
        block = lax.broadcasted_iota(jnp.int32, (GT, 256), 1) // SLOTS
        spread = jnp.zeros((GT, 256), F32)
        for d in range(NX):
            expert = 2 * lax.rem(x + d, NX) + half + EF * ab
            g = jnp.sum(jnp.where(lane == expert, share, 0.0), axis=1, keepdims=True)
            spread = jnp.where(block == d, g, spread)
        full = tu[ab, gam].astype(F32) * spread
        high = full.astype(BF16)
        thi[ab, gam] = high
        tlo[ab, gam] = (full - high.astype(F32)).astype(BF16)

    def x_copy(a, gam, d):
        return remote(
            xs.at[a, gam, d - 1], xr.at[a, gam, d], xss.at[a, gam, d - 1], xrs.at[a, gam, d - 1], dev(d, 0)
        )

    def xp_copy(a, gam, d):
        return remote(
            xps.at[a, gam, d - 1], xpr.at[a, gam, par, d], xpss.at[a, gam, d - 1], xprs.at[a, gam, d - 1], dev(d, 0)
        )

    def relay_copy(a, gam):
        part = xpr.at[a, gam, par, pl.ds(1, NX - 1)]
        return remote(part, part, rls.at[a, gam], rlr.at[a, gam], dev(0, mate_step))

    def tokens(a, c, gam, cols):
        return zb[a, c, pl.ds(GROUP * gam, GROUP), :, cols].reshape(GT, -1)

    def select(a, gam, before=None):
        ab = a // 2
        got = dot(tt[ab, gam, pl.ds(SLOTS, ROWS - SLOTS), :],
                  tokens(a, 0, gam, pl.ds(pl.multiple_of(par * W, LANES), W))).astype(BF16)
        for d in range(1, NX):
            xps[a, gam, d - 1] = got[SLOTS * (d - 1) : SLOTS * d]
        if before is not None:
            x_sent(*before)
        for d in (2, 1, 3):
            xp_copy(a, gam, d).start()
        for h in range(2):
            cols = pl.ds(h * W, W)
            got = dot(tt[ab, gam], tokens(a, 1, gam, cols)).astype(BF16)
            xr[a, gam, 0, :, cols] = got[:SLOTS]
            for d in range(1, NX):
                xs[a, gam, d - 1, :, cols] = got[SLOTS * d : SLOTS * (d + 1)]
        for d in (2, 1, 3):
            x_copy(a, gam, d).start()
        for h in range(2):
            got = dot(tt[ab, gam, pl.ds(0, SLOTS), :], tokens(a, 0, gam, pl.ds(h * W, W)))
            xpr[a, gam, h, 0] = got.astype(BF16)

    settled = set()

    def x_sent(a, gam):
        if ("x", a, gam) in settled:
            return
        settled.add(("x", a, gam))
        for d in range(1, NX):
            xp_copy(a, gam, d).wait_send()
            x_copy(a, gam, d).wait_send()

    def relay(a, gam):
        for d in range(1, NX):
            xp_copy(a, gam, d).wait_recv()
        relay_copy(a, gam).start()

    def x_wait(a, gam):
        for d in range(1, NX):
            x_copy(a, gam, d).wait_recv()
        relay_copy(a, gam).wait_recv()

    def rows_of(a, gam, j):
        if j < 2:
            return xpr[a, gam, j].reshape(ROWS, W)
        return xr[a, gam, :, :, pl.ds((j - 2) * W, W)].reshape(ROWS, W)

    def products(a, gam):
        acc = jnp.zeros((ROWS, 2 * FF), F32)
        for j in range(4):
            acc = acc + dot(rows_of(a, gam, j), wgu[pl.ds(j * W, W), :])
        return acc

    def y_copy(ab, gam, d):
        return remote(
            ys.at[ab, gam, d - 1], yr.at[ab, gam, pl.ds(SLOTS * d, SLOTS)],
            yss.at[ab, gam, d - 1], yrs.at[ab, gam, d - 1], dev(-d, 0),
        )

    def mate_copy(ab, gam):
        return remote(
            ypart.at[ab, gam, 1 - par], ymate.at[ab, gam], yms.at[ab, gam], ymr.at[ab, gam], dev(0, mate_step)
        )

    def ysum_copy(ab, gam, d):
        return remote(
            ysum.at[ab, gam, d - 1], ypr2.at[ab, gam, par, pl.ds(SLOTS * d, SLOTS)],
            yus.at[ab, gam, d - 1], yur.at[ab, gam, d - 1], dev(-d, 0),
        )

    def yp_copy(gam, d):
        return remote(
            yps.at[gam, d - 1], ypr.at[gam, pl.ds(SLOTS * d, SLOTS)],
            ypss.at[gam, d - 1], yprs.at[gam, d - 1], dev(-d, 0),
        )

    def send_back(ab, gam, left, product):
        for j in range(4):
            got = product(left, pl.ds(j * W, W)).astype(BF16)
            if j < 2:
                ypr2[ab, gam, j, pl.ds(0, SLOTS), :] = got[:SLOTS]
                for d in range(1, NX):
                    ypart[ab, gam, j, d - 1] = got[SLOTS * d : SLOTS * (d + 1)]
                if j == 1:
                    mate_copy(ab, gam).start()
            else:
                cols = pl.ds((j - 2) * W, W)
                yr[ab, gam, pl.ds(0, SLOTS), cols] = got[:SLOTS]
                for d in range(1, NX):
                    ys[ab, gam, d - 1, :, cols] = got[SLOTS * d : SLOTS * (d + 1)]

    def y_start(ab, gam):
        for d in (2, 1, 3):
            y_copy(ab, gam, d).start()

    def pair_start(ab, gam):
        mate_copy(ab, gam).wait_recv()
        for d in (2, 1, 3):
            both = ypart[ab, gam, par, d - 1].astype(F32) + ymate[ab, gam, d - 1].astype(F32)
            ysum[ab, gam, d - 1] = both.astype(BF16)
            ysum_copy(ab, gam, d).start()

    def y_sent(ab, gam):
        if ("y", ab, gam) in settled:
            return
        settled.add(("y", ab, gam))
        mate_copy(ab, gam).wait_send()
        for d in range(1, NX):
            y_copy(ab, gam, d).wait_send()
            ysum_copy(ab, gam, d).wait_send()

    def expert_backward(gam):
        uv = uvb[gam]
        u, v = uv[:, :FF], uv[:, FF:]
        q = jnp.zeros((ROWS, FF), F32)
        for j in range(4):
            q = q + dot_nt(rows_of(1, gam, j), wdv[:, pl.ds(j * W, W)])
        sig = sigmoid(u)
        act = (u * sig * v).astype(BF16)
        p = jnp.sum(act.astype(F32) * q, axis=1, keepdims=True)
        du = (q * v * sig * (1.0 + u * (1.0 - sig))).astype(BF16)
        dv = (q * u * sig).astype(BF16)
        own = lax.broadcasted_iota(jnp.int32, (ROWS, LANES), 1) == 2 * x + half
        pw = jnp.where(own, p, 0.0).astype(BF16)
        ypr[gam, pl.ds(0, SLOTS), :] = pw[:SLOTS]
        for d in range(1, NX):
            yps[gam, d - 1] = pw[SLOTS * d : SLOTS * (d + 1)]
            yp_copy(gam, d).start()
        send_back(0, gam, jnp.concatenate([du, dv], axis=1), lambda left, cols: dot_nt(left, wgu[cols, :]))

    def expert_forward(gam):
        uv = products(2, gam)
        u, v = uv[:, :FF], uv[:, FF:]
        act = (u * sigmoid(u) * v).astype(BF16)
        send_back(1, gam, act, lambda left, cols: dot(left, wdv[:, cols]))

    def combine(ab, gam):
        for d in range(1, NX):
            y_copy(ab, gam, d).wait_recv()
            ysum_copy(ab, gam, d).wait_recv()
        if ab == 0:
            for d in range(1, NX):
                yp_copy(gam, d).wait_recv()
            dots = dot(tu[0, gam], ypr[gam])
            centre = jnp.sum(gsh[gam] * dots, axis=1, keepdims=True)
            slope = (dots - centre) * gco[gam]
            slope_hi = slope.astype(BF16)
            slope_lo = (slope - slope_hi.astype(F32)).astype(BF16)
        for j in range(4):
            cols = pl.ds((j % 2) * W, W)
            rows = ypr2[ab, gam, j] if j < 2 else yr[ab, gam, :, cols]
            part = dot(thi[ab, gam], rows) + dot(tlo[ab, gam], rows)
            if ab == 0:
                centres = cpad[:, pl.ds(j * W, W)]
                part = part + dot(slope_hi, centres) + dot(slope_lo, centres)
            pacc[NC * ab + j // 2, pl.ds(GROUP * gam, GROUP), :, cols] = part.reshape(GROUP, TOK, W)

    def ring_copy(st, slot):
        i = slot - 1
        target = dev(0, -1) if slot % 2 == 1 else dev(0, 1)
        return remote(rss.at[st, i], rsr.at[st, i], rsss.at[st, i], rsrs.at[st, i], target)

    def ring_sum(streams, slots):
        for slot in slots:
            for st in streams:
                val = pacc[st, place_of(slot, par)]
                if slot + 2 < NZ:
                    ring_copy(st, slot + 2).wait_recv()
                    val = val + rsr[st, slot + 1].astype(F32)
                rss[st, slot - 1] = val.astype(BF16)
                ring_copy(st, slot).start()

    def ring_result(st):
        for slot in (1, 2):
            ring_copy(st, slot).wait_recv()
        return pacc[st, 0] + rsr[st, 0].astype(F32) + rsr[st, 1].astype(F32)

    for k in range(1, 5):
        z_step(0, k)
    z_start(1)
    table(0, 0)
    select(0, 0)
    shift.wait_recv()
    _, _, hf = normalize(rx[...])
    for c in range(NC):
        zb[2, c, 0] = hf[:, c * DC : (c + 1) * DC]
    for k in range(1, 5):
        z_step(0, k + 4)
        z_step(1, k)
    z_start(2)
    table(0, 1)
    select(0, 1)
    select(1, 0)
    relay(0, 0)
    for k in range(1, 5):
        z_step(1, k + 4)
        z_step(2, k)
    table(1, 0)
    select(1, 1)
    select(2, 0)
    relay(0, 1)
    relay(1, 0)
    table(1, 1)
    for k in range(5, 9):
        z_step(2, k)
    select(2, 1)
    relay(1, 1)

    for load in loads:
        load.wait()
    for gam in (0, 1):
        x_wait(0, gam)
        uvb[gam] = products(0, gam)
    relay(2, 0)
    for gam in (1, 0):
        x_wait(1, gam)
        expert_backward(gam)
        y_start(0, gam)
        if gam == 0:
            pair_start(0, 1)
    relay(2, 1)
    pair_start(0, 0)
    gates(0, 1)
    gates(0, 0)
    x_wait(2, 1)
    expert_forward(1)
    y_start(1, 1)
    x_wait(2, 0)
    expert_forward(0)
    pair_start(1, 1)
    y_start(1, 0)
    back = [0, 1]
    front = [2, 3]
    combine(0, 1)
    ring_sum(back, range(15, 12, -1))
    pair_start(1, 0)
    gates(1, 1)
    ring_sum(back, range(12, 10, -1))
    gates(1, 0)
    ring_sum(back, range(10, 8, -1))
    combine(0, 0)
    ring_sum(back, range(8, 4, -1))
    combine(1, 1)
    for slot in range(4, 0, -1):
        ring_sum(back, [slot])
        ring_sum(front, [slot + 11])
    ring_sum(front, range(11, 8, -1))
    combine(1, 0)
    ring_sum(front, range(8, 6, -1))
    xb, rb, _ = normalize(bx_ref[...])
    dh = jnp.concatenate([ring_result(0), ring_result(1)], axis=1) * ROUTE_SCALE
    proj = jnp.sum(dh * xb, axis=1, keepdims=True) * (1.0 / D)
    outb_ref[...] = (dy_ref[...].astype(F32) + rb * dh - rb * rb * rb * xb * proj).astype(BF16)

    ring_sum(front, range(6, 0, -1))
    for c in range(NC):
        cols = pl.ds(c * DC, DC)
        outf_ref[:, cols] = (rx[:, cols].astype(F32) + ROUTE_SCALE * ring_result(NC + c)).astype(BF16)

    shift.wait_send()
    for slot in range(1, NZ):
        for a in range(3):
            for piece in pieces(a):
                z_copy(*piece, slot).wait_send()
        for st in range(2 * NC):
            ring_copy(st, slot).wait_send()
    for gam in range(2):
        for a in range(3):
            x_sent(a, gam)
            relay_copy(a, gam).wait_send()
        for ab in range(2):
            y_sent(ab, gam)
        for d in range(1, NX):
            yp_copy(gam, d).wait_send()


def on_device(fwd_input, fwd_ids, bwd_input, bwd_ids, bwd_cot, centroids, w_gate, w_up, w_down):
    D = fwd_input.shape[-1]
    DC = D // NC
    W = DC // 2
    FF = w_gate.shape[-1]
    vmem = pl.BlockSpec(memory_space=pltpu.VMEM)
    anym = pl.BlockSpec(memory_space=pl.ANY)
    DMA = pltpu.SemaphoreType.DMA
    V = pltpu.VMEM
    outs = pl.pallas_call(
        kernel,
        out_shape=[jax.ShapeDtypeStruct((TOK, D), BF16)] * 2,
        in_specs=[vmem] * 6 + [anym] * 3,
        out_specs=[vmem] * 2,
        scratch_shapes=[
            V((D, 2 * FF), BF16),
            V((FF, D), BF16),
            V((LANES, D), BF16),
            V((TOK, D), BF16),
            V((NZ, TOK, LANES), BF16),
            V((3, NC, NZ, TOK, DC), BF16),
            V((2, 2, ROWS, GT), BF16),
            V((2, 2, GT, 256), BF16),
            V((2, 2, GT, 256), BF16),
            V((2, 2, GT, 256), BF16),
            V((3, 2, NX - 1, SLOTS, DC), BF16),
            V((3, 2, NX, SLOTS, DC), BF16),
            V((3, 2, NX - 1, SLOTS, W), BF16),
            V((3, 2, 2, NX, SLOTS, W), BF16),
            V((2, 2, 256, DC), BF16),
            V((2, 2, NX - 1, SLOTS, DC), BF16),
            V((2, 2, 2, NX - 1, SLOTS, W), BF16),
            V((2, 2, NX - 1, SLOTS, W), BF16),
            V((2, 2, NX - 1, SLOTS, W), BF16),
            V((2, 2, 2, 256, W), BF16),
            V((2, 256, LANES), BF16),
            V((2, NX - 1, SLOTS, LANES), BF16),
            V((2 * NC, NZ, TOK, DC), F32),
            V((2 * NC, NZ - 1, TOK, DC), BF16),
            V((2 * NC, NZ - 1, TOK, DC), BF16),
            V((2, ROWS, 2 * FF), F32),
            V((2, GT, LANES), F32),
            V((2, GT, LANES), F32),
            DMA((3,)),
            DMA,
            DMA,
            DMA((NZ - 1,)),
            DMA((NZ - 1,)),
            DMA((3, NC, NZ - 1)),
            DMA((3, NC, NZ - 1)),
            DMA((3, 2, NX - 1)),
            DMA((3, 2, NX - 1)),
            DMA((3, 2, NX - 1)),
            DMA((3, 2, NX - 1)),
            DMA((3, 2)),
            DMA((3, 2)),
            DMA((2, 2, NX - 1)),
            DMA((2, 2, NX - 1)),
            DMA((2, 2)),
            DMA((2, 2)),
            DMA((2, 2, NX - 1)),
            DMA((2, 2, NX - 1)),
            DMA((2, NX - 1)),
            DMA((2, NX - 1)),
            DMA((2 * NC, NZ - 1)),
            DMA((2 * NC, NZ - 1)),
        ],
        compiler_params=pltpu.CompilerParams(
            collective_id=0, has_side_effects=True, vmem_limit_bytes=60 * 2**20
        ),
        cost_estimate=pl.CostEstimate(flops=6 * 10**9, bytes_accessed=4 * 10**6, transcendentals=0),
        name="expert_layer",
    )(
        fwd_input[0], fwd_ids[0], bwd_input[0], bwd_ids[0], bwd_cot[0], centroids[0],
        w_gate[0], w_up[0], w_down[0],
    )
    return outs[0][None], outs[1][None]


def solution(mesh):
    return jax.shard_map(
        on_device,
        mesh=mesh,
        in_specs=(
            P("section", "expert", None),
            P("section", "expert", None),
            P("section", "expert", None),
            P("section", "expert", None),
            P("section", "expert", None),
            P("section", None, None),
            P("section", None, "expert"),
            P("section", None, "expert"),
            P("section", "expert", None),
        ),
        out_specs=(P("section", "expert", None), P("section", "expert", None)),
        check_vma=False,
    )
```

```python
import functools

import jax
import jax.numpy as jnp
from jax import lax
from jax.experimental import pallas as pl
from jax.experimental.pallas import tpu as pltpu
from jax.sharding import PartitionSpec as P

MESH = pl.DeviceIdType.MESH
EF = 8
CAP = 6
NX = 4
NZ = 16
TOK = 16
EPS = 1e-06
ROUTE_SCALE = 2.5
NC = 2
GROUP = NZ // 2
SLOTS = GROUP * CAP
ROWS = NX * SLOTS
GT = GROUP * TOK
LANES = 128
STEP = 256
F32 = jnp.float32
BF16 = jnp.bfloat16
NT = (((1,), (1,)), ((), ()))


def dot(a, b):
    return jnp.dot(a, b, preferred_element_type=F32)


def dot_nt(a, b):
    return lax.dot_general(a, b, NT, preferred_element_type=F32)


def sigmoid(v):
    return jax.nn.sigmoid(v)


def kernel(
    fx_ref, fid_ref, bx_ref, bid_ref, dy_ref, cent_ref, wg_ref, wu_ref, wd_ref,
    outf_ref, outb_ref,
    wgu, wdv, cpad, rx, zm, zb, tt, tu, thi, tlo, xs, xr, xps, xpr, yr, ys, ypart, ymate, ysum, ypr2, ypr, yps,
    pacc, rss, rsr, uvb, gsh, gco,
    wsem, shs, shr, zms, zmr, zs, zr, xss, xrs, xpss, xprs, rls, rlr, yss, yrs, yms, ymr, yus, yur, ypss, yprs,
    rsss, rsrs,
):
    D = fx_ref.shape[-1]
    DC = D // NC
    W = DC // 2
    FF = wdv.shape[0]
    sec = lax.axis_index("section")
    nsec = lax.axis_size("section")
    pos_e = lax.axis_index("expert")
    x = pos_e // NZ
    z = lax.rem(pos_e, NZ)
    half = z // GROUP
    par = lax.rem(z, 2)
    mate_step = 1 - 2 * par

    def dev(dx, dz, ds=0):
        xx = lax.rem(x + dx + NX, NX)
        zz = lax.rem(z + dz + NZ, NZ)
        return (lax.rem(sec + ds + nsec, nsec), xx * NZ + zz)

    def remote(src, dst, ss, rs, device):
        return pltpu.make_async_remote_copy(
            src_ref=src, dst_ref=dst, send_sem=ss, recv_sem=rs, device_id=device, device_id_type=MESH
        )

    barrier = pltpu.get_barrier_semaphore()
    partners = [dev(0, 1), dev(0, -1), dev(1, 0), dev(2, 0), dev(3, 0), dev(0, 0, 1), dev(0, 0, -1)]
    for partner in partners:
        pl.semaphore_signal(barrier, inc=1, device_id=partner, device_id_type=MESH)

    loads = [
        pltpu.make_async_copy(wg_ref, wgu.at[:, pl.ds(0, FF)], wsem.at[0]),
        pltpu.make_async_copy(wu_ref, wgu.at[:, pl.ds(FF, FF)], wsem.at[1]),
        pltpu.make_async_copy(wd_ref, wdv, wsem.at[2]),
    ]
    for load in loads:
        load.start()

    lane16 = lax.broadcasted_iota(jnp.int32, (TOK, LANES), 1)
    chosen = (lane16 == bid_ref[:, 0:1]) | (lane16 == bid_ref[:, 1:2])
    chosen = chosen | (lane16 == fid_ref[:, 0:1] + EF) | (lane16 == fid_ref[:, 1:2] + EF)
    zm[0] = jnp.where(chosen, 1.0, 0.0).astype(BF16)

    def normalize(v):
        wide = v.astype(F32)
        inv = lax.rsqrt(jnp.sum(wide * wide, axis=-1, keepdims=True) * (1.0 / D) + EPS)
        return wide, inv, (wide * inv).astype(BF16)

    _, _, hb = normalize(bx_ref[...])
    for c in range(NC):
        zb[0, c, 0] = hb[:, c * DC : (c + 1) * DC]
        zb[1, c, 0] = dy_ref[:, c * DC : (c + 1) * DC]

    pl.semaphore_wait(barrier, len(partners))

    def place_of(slot, parity):
        return 8 - parity if slot == 7 else 7 + parity if slot == 8 else slot

    def z_copy(a, c, slot):
        src = 0 if slot <= 2 else place_of(slot - 2, par)
        dst = place_of(slot, 1 - par)
        target = dev(0, 1) if slot % 2 == 1 else dev(0, -1)
        if a < 0:
            return remote(zm.at[src], zm.at[dst], zms.at[slot - 1], zmr.at[slot - 1], target)
        return remote(zb.at[a, c, src], zb.at[a, c, dst], zs.at[a, c, slot - 1], zr.at[a, c, slot - 1], target)

    def pieces(a):
        return [(-1, 0), (0, 0), (0, 1)] if a == 0 else [(a, c) for c in range(NC)]

    def z_start(a):
        for piece in pieces(a):
            for slot in (1, 2):
                z_copy(*piece, slot).start()

    def z_step(a, k):
        for piece in pieces(a):
            for slot in (2 * k - 1, 2 * k):
                if slot < NZ:
                    z_copy(*piece, slot).wait_recv()
                    if slot + 2 < NZ:
                        z_copy(*piece, slot + 2).start()

    z_start(0)
    shift = remote(fx_ref, rx, shs, shr, dev(0, 0, 1))
    shift.start()

    cpad[...] = jnp.zeros_like(cpad)
    cpad[pl.ds(0, 2 * EF), :] = jnp.concatenate([cent_ref[...], cent_ref[...]], axis=0)
    for ab in range(2):
        for gam in range(2):
            yr[ab, gam, pl.ds(ROWS, 256 - ROWS), :] = jnp.zeros((256 - ROWS, DC), BF16)
            ypr2[ab, gam, par, pl.ds(ROWS, 256 - ROWS), :] = jnp.zeros((256 - ROWS, W), BF16)
            ypr2[ab, gam, 1 - par, pl.ds(SLOTS, 256 - SLOTS), :] = jnp.zeros((256 - SLOTS, W), BF16)
    for gam in range(2):
        ypr[gam, pl.ds(ROWS, 256 - ROWS), :] = jnp.zeros((256 - ROWS, LANES), BF16)

    lane = lax.broadcasted_iota(jnp.int32, (GT, LANES), 1)

    def away(place, parity):
        if place in (7, 8):
            return -4 if (place == 7) == (parity == 1) else 4
        return place // 2 if place % 2 == 0 else -(place + 1) // 2

    def table(ab, gam):
        mask = zm[pl.ds(GROUP * gam, GROUP)].reshape(GT, LANES)
        row_i = lax.broadcasted_iota(jnp.int32, (GT, GT), 0)
        col_i = lax.broadcasted_iota(jnp.int32, (GT, GT), 1)
        below = jnp.where((row_i // TOK == col_i // TOK) & (col_i < row_i), 1.0, 0.0).astype(BF16)
        place = dot(below, mask)
        maskf = mask.astype(F32)
        block = lax.broadcasted_iota(jnp.int32, (GT, 1), 0) // TOK
        order = jnp.zeros((GT, 1), jnp.int32)
        for b in range(GROUP):
            even, odd = [(away(b + GROUP * gam, parity) + parity + 3 - GROUP * gam) % NZ for parity in (0, 1)]
            order = jnp.where(block == b, even + (odd - even) * par, order)
        base = (order * CAP).astype(F32)
        wide_lane = lax.broadcasted_iota(jnp.int32, (GT, 256), 1).astype(F32)
        total = jnp.zeros((GT, 256), F32)
        for d in range(NX):
            expert = 2 * lax.rem(x + d, NX) + half + EF * ab
            pick = lane == expert
            named = jnp.sum(jnp.where(pick, maskf, 0.0), axis=1, keepdims=True)
            slot = jnp.sum(jnp.where(pick, place, 0.0), axis=1, keepdims=True) + base + float(SLOTS * d)
            total = total + jnp.where(wide_lane == slot, named, 0.0)
        tu[ab, gam] = total.astype(BF16)
        tt[ab, gam] = total.T[:ROWS].astype(BF16)

    def gates_of(logits, mask, ab, width):
        inside = (width >= EF * ab) & (width < EF * (ab + 1)) & (mask > 0)
        aff = sigmoid(logits)
        picked = jnp.where(inside, aff, 0.0)
        denom = jnp.sum(picked, axis=1, keepdims=True)
        return inside, aff, denom, picked / denom

    def gates(ab, gam):
        a = 2 * ab
        acc = jnp.zeros((GT, LANES), F32)
        for c in range(NC):
            def add(k, acc, c=c):
                col = pl.multiple_of(k * STEP, STEP)
                rows = zb[a, c, pl.ds(GROUP * gam, GROUP), :, pl.ds(col, STEP)].reshape(GT, STEP)
                return acc + dot_nt(rows, cpad[:, pl.ds(c * DC + col, STEP)])
            acc = lax.fori_loop(0, DC // STEP, add, acc)
        mask = zm[pl.ds(GROUP * gam, GROUP)].reshape(GT, LANES).astype(F32)
        inside, aff, denom, share = gates_of(acc, mask, ab, lane)
        if ab == 0:
            gsh[gam] = share
            gco[gam] = jnp.where(inside, aff * (1.0 - aff) / denom, 0.0)
        block = lax.broadcasted_iota(jnp.int32, (GT, 256), 1) // SLOTS
        spread = jnp.zeros((GT, 256), F32)
        for d in range(NX):
            expert = 2 * lax.rem(x + d, NX) + half + EF * ab
            g = jnp.sum(jnp.where(lane == expert, share, 0.0), axis=1, keepdims=True)
            spread = jnp.where(block == d, g, spread)
        full = tu[ab, gam].astype(F32) * spread
        high = full.astype(BF16)
        thi[ab, gam] = high
        tlo[ab, gam] = (full - high.astype(F32)).astype(BF16)

    def x_copy(a, gam, d):
        return remote(
            xs.at[a, gam, d - 1], xr.at[a, gam, d], xss.at[a, gam, d - 1], xrs.at[a, gam, d - 1], dev(d, 0)
        )

    def xp_copy(a, gam, d):
        return remote(
            xps.at[a, gam, d - 1], xpr.at[a, gam, par, d], xpss.at[a, gam, d - 1], xprs.at[a, gam, d - 1], dev(d, 0)
        )

    def relay_copy(a, gam):
        part = xpr.at[a, gam, par, pl.ds(1, NX - 1)]
        return remote(part, part, rls.at[a, gam], rlr.at[a, gam], dev(0, mate_step))

    def tokens(a, c, gam, cols):
        return zb[a, c, pl.ds(GROUP * gam, GROUP), :, cols].reshape(GT, -1)

    def select(a, gam, before=None):
        ab = a // 2
        got = dot(tt[ab, gam, pl.ds(SLOTS, ROWS - SLOTS), :],
                  tokens(a, 0, gam, pl.ds(pl.multiple_of(par * W, LANES), W))).astype(BF16)
        for d in range(1, NX):
            xps[a, gam, d - 1] = got[SLOTS * (d - 1) : SLOTS * d]
        if before is not None:
            x_sent(*before)
        for d in (2, 1, 3):
            xp_copy(a, gam, d).start()
        for h in range(2):
            cols = pl.ds(h * W, W)
            got = dot(tt[ab, gam], tokens(a, 1, gam, cols)).astype(BF16)
            xr[a, gam, 0, :, cols] = got[:SLOTS]
            for d in range(1, NX):
                xs[a, gam, d - 1, :, cols] = got[SLOTS * d : SLOTS * (d + 1)]
        for d in (2, 1, 3):
            x_copy(a, gam, d).start()
        for h in range(2):
            got = dot(tt[ab, gam, pl.ds(0, SLOTS), :], tokens(a, 0, gam, pl.ds(h * W, W)))
            xpr[a, gam, h, 0] = got.astype(BF16)

    settled = set()

    def x_sent(a, gam):
        if ("x", a, gam) in settled:
            return
        settled.add(("x", a, gam))
        for d in range(1, NX):
            xp_copy(a, gam, d).wait_send()
            x_copy(a, gam, d).wait_send()

    def relay(a, gam):
        for d in range(1, NX):
            xp_copy(a, gam, d).wait_recv()
        relay_copy(a, gam).start()

    def x_wait(a, gam):
        for d in range(1, NX):
            x_copy(a, gam, d).wait_recv()
        relay_copy(a, gam).wait_recv()

    def rows_of(a, gam, j):
        if j < 2:
            return xpr[a, gam, j].reshape(ROWS, W)
        return xr[a, gam, :, :, pl.ds((j - 2) * W, W)].reshape(ROWS, W)

    def products(a, gam):
        acc = jnp.zeros((ROWS, 2 * FF), F32)
        for j in range(4):
            acc = acc + dot(rows_of(a, gam, j), wgu[pl.ds(j * W, W), :])
        return acc

    def y_copy(ab, gam, d):
        return remote(
            ys.at[ab, gam, d - 1], yr.at[ab, gam, pl.ds(SLOTS * d, SLOTS)],
            yss.at[ab, gam, d - 1], yrs.at[ab, gam, d - 1], dev(-d, 0),
        )

    def mate_copy(ab, gam):
        return remote(
            ypart.at[ab, gam, 1 - par], ymate.at[ab, gam], yms.at[ab, gam], ymr.at[ab, gam], dev(0, mate_step)
        )

    def ysum_copy(ab, gam, d):
        return remote(
            ysum.at[ab, gam, d - 1], ypr2.at[ab, gam, par, pl.ds(SLOTS * d, SLOTS)],
            yus.at[ab, gam, d - 1], yur.at[ab, gam, d - 1], dev(-d, 0),
        )

    def yp_copy(gam, d):
        return remote(
            yps.at[gam, d - 1], ypr.at[gam, pl.ds(SLOTS * d, SLOTS)],
            ypss.at[gam, d - 1], yprs.at[gam, d - 1], dev(-d, 0),
        )

    def send_back(ab, gam, left, product):
        for j in range(4):
            got = product(left, pl.ds(j * W, W)).astype(BF16)
            if j < 2:
                ypr2[ab, gam, j, pl.ds(0, SLOTS), :] = got[:SLOTS]
                for d in range(1, NX):
                    ypart[ab, gam, j, d - 1] = got[SLOTS * d : SLOTS * (d + 1)]
                if j == 1:
                    mate_copy(ab, gam).start()
            else:
                cols = pl.ds((j - 2) * W, W)
                yr[ab, gam, pl.ds(0, SLOTS), cols] = got[:SLOTS]
                for d in range(1, NX):
                    ys[ab, gam, d - 1, :, cols] = got[SLOTS * d : SLOTS * (d + 1)]

    def y_start(ab, gam):
        for d in (2, 1, 3):
            y_copy(ab, gam, d).start()

    def pair_start(ab, gam):
        mate_copy(ab, gam).wait_recv()
        for d in (2, 1, 3):
            both = ypart[ab, gam, par, d - 1].astype(F32) + ymate[ab, gam, d - 1].astype(F32)
            ysum[ab, gam, d - 1] = both.astype(BF16)
            ysum_copy(ab, gam, d).start()

    def y_sent(ab, gam):
        if ("y", ab, gam) in settled:
            return
        settled.add(("y", ab, gam))
        mate_copy(ab, gam).wait_send()
        for d in range(1, NX):
            y_copy(ab, gam, d).wait_send()
            ysum_copy(ab, gam, d).wait_send()

    def expert_backward(gam):
        uv = uvb[gam]
        u, v = uv[:, :FF], uv[:, FF:]
        q = jnp.zeros((ROWS, FF), F32)
        for j in range(4):
            q = q + dot_nt(rows_of(1, gam, j), wdv[:, pl.ds(j * W, W)])
        sig = sigmoid(u)
        act = (u * sig * v).astype(BF16)
        p = jnp.sum(act.astype(F32) * q, axis=1, keepdims=True)
        du = (q * v * sig * (1.0 + u * (1.0 - sig))).astype(BF16)
        dv = (q * u * sig).astype(BF16)
        own = lax.broadcasted_iota(jnp.int32, (ROWS, LANES), 1) == 2 * x + half
        pw = jnp.where(own, p, 0.0).astype(BF16)
        ypr[gam, pl.ds(0, SLOTS), :] = pw[:SLOTS]
        for d in range(1, NX):
            yps[gam, d - 1] = pw[SLOTS * d : SLOTS * (d + 1)]
            yp_copy(gam, d).start()
        send_back(0, gam, jnp.concatenate([du, dv], axis=1), lambda left, cols: dot_nt(left, wgu[cols, :]))

    def expert_forward(gam):
        uv = products(2, gam)
        u, v = uv[:, :FF], uv[:, FF:]
        act = (u * sigmoid(u) * v).astype(BF16)
        send_back(1, gam, act, lambda left, cols: dot(left, wdv[:, cols]))

    def combine(ab, gam):
        for d in range(1, NX):
            y_copy(ab, gam, d).wait_recv()
            ysum_copy(ab, gam, d).wait_recv()
        if ab == 0:
            for d in range(1, NX):
                yp_copy(gam, d).wait_recv()
            dots = dot(tu[0, gam], ypr[gam])
            centre = jnp.sum(gsh[gam] * dots, axis=1, keepdims=True)
            slope = (dots - centre) * gco[gam]
            slope_hi = slope.astype(BF16)
            slope_lo = (slope - slope_hi.astype(F32)).astype(BF16)
        for j in range(4):
            cols = pl.ds((j % 2) * W, W)
            rows = ypr2[ab, gam, j] if j < 2 else yr[ab, gam, :, cols]
            part = dot(thi[ab, gam], rows) + dot(tlo[ab, gam], rows)
            if ab == 0:
                centres = cpad[:, pl.ds(j * W, W)]
                part = part + dot(slope_hi, centres) + dot(slope_lo, centres)
            pacc[NC * ab + j // 2, pl.ds(GROUP * gam, GROUP), :, cols] = part.reshape(GROUP, TOK, W)

    def ring_copy(st, slot):
        i = slot - 1
        target = dev(0, -1) if slot % 2 == 1 else dev(0, 1)
        return remote(rss.at[st, i], rsr.at[st, i], rsss.at[st, i], rsrs.at[st, i], target)

    def ring_sum(streams, slots):
        for slot in slots:
            for st in streams:
                val = pacc[st, place_of(slot, par)]
                if slot + 2 < NZ:
                    ring_copy(st, slot + 2).wait_recv()
                    val = val + rsr[st, slot + 1].astype(F32)
                rss[st, slot - 1] = val.astype(BF16)
                ring_copy(st, slot).start()

    def ring_result(st):
        for slot in (1, 2):
            ring_copy(st, slot).wait_recv()
        return pacc[st, 0] + rsr[st, 0].astype(F32) + rsr[st, 1].astype(F32)

    for k in range(1, 5):
        z_step(0, k)
    z_start(1)
    table(0, 0)
    select(0, 0)
    shift.wait_recv()
    _, _, hf = normalize(rx[...])
    for c in range(NC):
        zb[2, c, 0] = hf[:, c * DC : (c + 1) * DC]
    for k in range(1, 5):
        z_step(0, k + 4)
        z_step(1, k)
    z_start(2)
    table(0, 1)
    select(0, 1)
    select(1, 0)
    relay(0, 0)
    for k in range(1, 5):
        z_step(1, k + 4)
        z_step(2, k)
    table(1, 0)
    select(1, 1)
    select(2, 0)
    relay(0, 1)
    relay(1, 0)
    table(1, 1)
    for k in range(5, 9):
        z_step(2, k)
    select(2, 1)
    relay(1, 1)

    for load in loads:
        load.wait()
    for gam in (0, 1):
        x_wait(0, gam)
        uvb[gam] = products(0, gam)
    relay(2, 0)
    for gam in (1, 0):
        x_wait(1, gam)
        expert_backward(gam)
        y_start(0, gam)
        if gam == 0:
            pair_start(0, 1)
    relay(2, 1)
    pair_start(0, 0)
    gates(0, 1)
    gates(0, 0)
    x_wait(2, 1)
    expert_forward(1)
    y_start(1, 1)
    x_wait(2, 0)
    expert_forward(0)
    pair_start(1, 1)
    y_start(1, 0)
    back = [0, 1]
    front = [2, 3]
    combine(0, 1)
    ring_sum(back, range(15, 14, -1))
    pair_start(1, 0)
    ring_sum(back, range(14, 12, -1))
    gates(1, 1)
    ring_sum(back, range(12, 10, -1))
    gates(1, 0)
    ring_sum(back, range(10, 8, -1))
    combine(0, 0)
    ring_sum(back, range(8, 6, -1))
    combine(1, 1)
    ring_sum(front, [15])
    for slot in range(6, 0, -1):
        ring_sum(back, [slot])
        ring_sum(front, [slot + 8])
    combine(1, 0)
    ring_sum(front, range(8, 6, -1))
    xb, rb, _ = normalize(bx_ref[...])
    dh = jnp.concatenate([ring_result(0), ring_result(1)], axis=1) * ROUTE_SCALE
    proj = jnp.sum(dh * xb, axis=1, keepdims=True) * (1.0 / D)
    outb_ref[...] = (dy_ref[...].astype(F32) + rb * dh - rb * rb * rb * xb * proj).astype(BF16)

    ring_sum(front, range(6, 0, -1))
    for c in range(NC):
        cols = pl.ds(c * DC, DC)
        outf_ref[:, cols] = (rx[:, cols].astype(F32) + ROUTE_SCALE * ring_result(NC + c)).astype(BF16)

    shift.wait_send()
    for slot in range(1, NZ):
        for a in range(3):
            for piece in pieces(a):
                z_copy(*piece, slot).wait_send()
        for st in range(2 * NC):
            ring_copy(st, slot).wait_send()
    for gam in range(2):
        for a in range(3):
            x_sent(a, gam)
            relay_copy(a, gam).wait_send()
        for ab in range(2):
            y_sent(ab, gam)
        for d in range(1, NX):
            yp_copy(gam, d).wait_send()


def on_device(fwd_input, fwd_ids, bwd_input, bwd_ids, bwd_cot, centroids, w_gate, w_up, w_down):
    D = fwd_input.shape[-1]
    DC = D // NC
    W = DC // 2
    FF = w_gate.shape[-1]
    vmem = pl.BlockSpec(memory_space=pltpu.VMEM)
    anym = pl.BlockSpec(memory_space=pl.ANY)
    DMA = pltpu.SemaphoreType.DMA
    V = pltpu.VMEM
    outs = pl.pallas_call(
        kernel,
        out_shape=[jax.ShapeDtypeStruct((TOK, D), BF16)] * 2,
        in_specs=[vmem] * 6 + [anym] * 3,
        out_specs=[vmem] * 2,
        scratch_shapes=[
            V((D, 2 * FF), BF16),
            V((FF, D), BF16),
            V((LANES, D), BF16),
            V((TOK, D), BF16),
            V((NZ, TOK, LANES), BF16),
            V((3, NC, NZ, TOK, DC), BF16),
            V((2, 2, ROWS, GT), BF16),
            V((2, 2, GT, 256), BF16),
            V((2, 2, GT, 256), BF16),
            V((2, 2, GT, 256), BF16),
            V((3, 2, NX - 1, SLOTS, DC), BF16),
            V((3, 2, NX, SLOTS, DC), BF16),
            V((3, 2, NX - 1, SLOTS, W), BF16),
            V((3, 2, 2, NX, SLOTS, W), BF16),
            V((2, 2, 256, DC), BF16),
            V((2, 2, NX - 1, SLOTS, DC), BF16),
            V((2, 2, 2, NX - 1, SLOTS, W), BF16),
            V((2, 2, NX - 1, SLOTS, W), BF16),
            V((2, 2, NX - 1, SLOTS, W), BF16),
            V((2, 2, 2, 256, W), BF16),
            V((2, 256, LANES), BF16),
            V((2, NX - 1, SLOTS, LANES), BF16),
            V((2 * NC, NZ, TOK, DC), F32),
            V((2 * NC, NZ - 1, TOK, DC), BF16),
            V((2 * NC, NZ - 1, TOK, DC), BF16),
            V((2, ROWS, 2 * FF), F32),
            V((2, GT, LANES), F32),
            V((2, GT, LANES), F32),
            DMA((3,)),
            DMA,
            DMA,
            DMA((NZ - 1,)),
            DMA((NZ - 1,)),
            DMA((3, NC, NZ - 1)),
            DMA((3, NC, NZ - 1)),
            DMA((3, 2, NX - 1)),
            DMA((3, 2, NX - 1)),
            DMA((3, 2, NX - 1)),
            DMA((3, 2, NX - 1)),
            DMA((3, 2)),
            DMA((3, 2)),
            DMA((2, 2, NX - 1)),
            DMA((2, 2, NX - 1)),
            DMA((2, 2)),
            DMA((2, 2)),
            DMA((2, 2, NX - 1)),
            DMA((2, 2, NX - 1)),
            DMA((2, NX - 1)),
            DMA((2, NX - 1)),
            DMA((2 * NC, NZ - 1)),
            DMA((2 * NC, NZ - 1)),
        ],
        compiler_params=pltpu.CompilerParams(
            collective_id=0, has_side_effects=True, vmem_limit_bytes=60 * 2**20
        ),
        cost_estimate=pl.CostEstimate(flops=6 * 10**9, bytes_accessed=4 * 10**6, transcendentals=0),
        name="expert_layer",
    )(
        fwd_input[0], fwd_ids[0], bwd_input[0], bwd_ids[0], bwd_cot[0], centroids[0],
        w_gate[0], w_up[0], w_down[0],
    )
    return outs[0][None], outs[1][None]


def solution(mesh):
    return jax.shard_map(
        on_device,
        mesh=mesh,
        in_specs=(
            P("section", "expert", None),
            P("section", "expert", None),
            P("section", "expert", None),
            P("section", "expert", None),
            P("section", "expert", None),
            P("section", None, None),
            P("section", None, "expert"),
            P("section", None, "expert"),
            P("section", "expert", None),
        ),
        out_specs=(P("section", "expert", None), P("section", "expert", None)),
        check_vma=False,
    )
```
